256 devices in a mesh: frame: 8 (over y_lo, x), row: 32 (over y_hi, z, core).
Axes of the slice: x: 4, y: 4 (y_hi: 2, y_lo: 2; y = y_hi * 2 + y_lo), z: 8, core: 2. Of those that a mesh axis runs over, the one named last changes fastest.
Arguments:
- latent: float32 [16, 64, 320, 128], P('frame', 'row'), may hold values from -51 to 51
- cotangent: float32 [16, 64, 320, 128], P('frame', 'row'), may hold values from -6 to 6
- gn_gain: float32 [320], replicated, may hold values from 0.1 to 1.9
- gn_bias: float32 [320], replicated, may hold values from -3 to 3
- w_spatial: float32 [3, 3, 320, 320], replicated, may hold values from -0.109375 to 0.109375
- w_temporal: float32 [3, 320, 320], replicated, may hold values from -0.1875 to 0.1875
- ln_gain: float32 [320], replicated, may hold values from 0.1 to 1.9
- ln_bias: float32 [320], replicated, may hold values from -3 to 3
- w_query: float32 [320, 320], replicated, may hold values from -1.5 to 1.5
- w_key: float32 [320, 320], replicated, may hold values from -1.5 to 1.5
- w_value: float32 [320, 320], replicated, may hold values from -0.3125 to 0.3125
- w_out: float32 [320, 320], replicated, may hold values from -0.3125 to 0.3125
Outputs:
- output: float32 [16, 64, 320, 128], P('frame', 'row')
- grad_latent: float32 [16, 64, 320, 128], P('frame', 'row')
The draws below stay inside these ranges and needn't reach their ends.
All inputs are finite; a program needn't handle non-finite values.
Results may differ from the reference program's by a relative error of at most 0.0003.
Values sent between devices are 32-bit elements; how exact they have to be, the bound alone decides.
A program may use at most 128 MiB of HBM per device.

```python
import math
import jax
import jax.numpy as jnp
from jax import lax

C = 320
GROUPS = 32
HEADS = 5
HEAD_DIM = 64
COLS = 128
FRAMES = 16
ROWS = 64


def draw_latent(key, part):
    key = jax.random.fold_in(key, 1)
    base_key, row_key, chan_key = jax.random.split(key, 3)
    shape = (FRAMES, ROWS, C, COLS)
    base = jnp.clip(jax.random.normal(base_key, shape, jnp.float32), -4.0, 4.0)
    position = jnp.arange(ROWS, dtype=jnp.float32) / max(ROWS - 1, 1)
    row_scale = jnp.exp(math.log(3.0) * position) * jax.random.uniform(row_key, (ROWS,), jnp.float32, 0.7, 1.4)
    chan_scale = jnp.exp(jax.random.uniform(chan_key, (C,), jnp.float32, math.log(0.3), math.log(3.0)))
    return base * row_scale[None, :, None, None] * chan_scale[None, None, :, None]


def shared_weight(key):
    return jnp.clip(jax.random.normal(key, (C, C), jnp.float32), -4.0, 4.0)


def draw_w_query(key, part):
    common = shared_weight(key)
    key = jax.random.fold_in(key, 2)
    own = jnp.clip(jax.random.normal(key, (C, C), jnp.float32), -4.0, 4.0)
    return jnp.clip(0.02 * common + own * C ** (-0.5), -1.5, 1.5)


def draw_w_key(key, part):
    common = shared_weight(key)
    key = jax.random.fold_in(key, 3)
    own = jnp.clip(jax.random.normal(key, (C, C), jnp.float32), -4.0, 4.0)
    return jnp.clip(0.02 * common + own * C ** (-0.5), -1.5, 1.5)


def levels(own_key, shape, cuts, least, high):
    def one(axis_at, shards_of):
        draws = jax.random.uniform(jax.random.fold_in(jax.random.fold_in(own_key, 6), axis_at), (shards_of,), jnp.float32, least / len(cuts), high / len(cuts))
        return jnp.repeat(jnp.exp(draws), shape[axis_at] // shards_of).reshape((-1,) + (1,) * (len(shape) - axis_at - 1))

    factor_of = one(*cuts[0])
    for cut in cuts[1:]:
        factor_of = factor_of * one(*cut)
    return factor_of


def centred(stream_key, dims, scale, most, cuts=(), kind=jnp.bfloat16):
    values = jax.random.normal(stream_key, dims, jnp.float32) * scale
    if len(cuts) > 0:
        values = levels(stream_key, dims, cuts, -0.22, 0.18) * values
    return jnp.clip(values, min=-most, max=most).astype(kind)


def setup_inputs(seed: int = 0) -> dict:
    streams_of = jax.random.split(jax.random.key(seed), 13)
    return {
        "latent": draw_latent(jax.random.fold_in(streams_of[12], 71), 0),
        "cotangent": centred(streams_of[1], (FRAMES, ROWS, C, COLS), 1.0, 6.0, ((0, 8), (1, 32)), jnp.float32),
        "gn_gain": jnp.clip(1.0 + 0.18 * jax.random.normal(streams_of[2], (C,), jnp.float32), 0.1, 1.9),
        "gn_bias": centred(streams_of[3], (C,), 0.5, 3.0, (), jnp.float32),
        "w_spatial": centred(streams_of[4], (3, 3, C, C), (9 * C) ** -0.5, 0.109375, (), jnp.float32),
        "w_temporal": centred(streams_of[5], (3, C, C), (3 * C) ** -0.5, 0.1875, (), jnp.float32),
        "ln_gain": jnp.clip(1.0 + 0.18 * jax.random.normal(streams_of[6], (C,), jnp.float32), 0.1, 1.9),
        "ln_bias": centred(streams_of[7], (C,), 0.5, 3.0, (), jnp.float32),
        "w_query": draw_w_query(jax.random.fold_in(streams_of[12], 71), 0),
        "w_key": draw_w_key(jax.random.fold_in(streams_of[12], 71), 0),
        "w_value": centred(streams_of[10], (C, C), C ** -0.5, 0.3125, (), jnp.float32),
        "w_out": centred(streams_of[11], (C, C), C ** -0.5, 0.3125, (), jnp.float32),
    }


HIGHEST = lax.Precision.HIGHEST
EPSILON = 1e-05

def mix(values, weight):
    return jnp.einsum('frcw,cd->frdw', values, weight, precision=HIGHEST)

def spatial_sweep(padded, kernel):
    height = padded.shape[1] - 2
    width = padded.shape[3] - 2
    total = None
    for across in range(3):
        for along in range(3):
            term = mix(padded[:, across:across + height, :, along:along + width], kernel[across, along])
            total = term if total is None else total + term
    return total

def temporal_sweep(padded, kernel):
    count = padded.shape[0] - 2
    total = None
    for offset in range(3):
        term = mix(padded[offset:offset + count], kernel[offset])
        total = term if total is None else total + term
    return total

def group_apply(values, mean, rstd, gain, bias):
    frames, height, chans, width = values.shape
    grouped = values.reshape(frames, height, GROUPS, chans // GROUPS, width)
    normal = (grouped - mean[:, None, :, None, None]) * rstd[:, None, :, None, None]
    normal = normal.reshape(frames, height, chans, width)
    return (normal, normal * gain[None, None, :, None] + bias[None, None, :, None])

def layer_stats(values, gain, bias):
    centre = lax.optimization_barrier(jnp.mean(values, axis=2, keepdims=True))
    centered = values - centre
    spread = lax.optimization_barrier(jnp.mean(centered * centered, axis=2, keepdims=True))
    rstd = lax.rsqrt(spread + EPSILON)
    normal = centered * rstd
    return (normal * gain[None, None, :, None] + bias[None, None, :, None], normal, rstd)

def split_heads(values):
    frames, height, chans, width = values.shape
    return values.reshape(frames, height, HEADS, HEAD_DIM, width)

def attend(query, keys, values):
    scores = jnp.einsum('frhdp,grhdp->frhpg', split_heads(query), split_heads(keys), precision=HIGHEST) * HEAD_DIM ** (-0.5)
    weights = jax.nn.softmax(scores, axis=-1)
    mixed = jnp.einsum('frhpg,grhdp->frhdp', weights, split_heads(values), precision=HIGHEST)
    return (mixed.reshape(query.shape), weights)

def block(latent, gn_gain, gn_bias, w_spatial, w_temporal, ln_gain, ln_bias, w_query, w_key, w_value, w_out):
    frames, height, chans, width = latent.shape
    grouped = latent.reshape(frames, height, GROUPS, chans // GROUPS, width)
    members = height * (chans // GROUPS) * width
    group_mean = lax.optimization_barrier(jnp.sum(grouped, axis=(1, 3, 4))) / members
    group_rstd = lax.rsqrt(lax.optimization_barrier(jnp.sum(grouped * grouped, axis=(1, 3, 4))) / members - group_mean * group_mean + EPSILON)
    shifted = group_apply(latent, group_mean, group_rstd, gn_gain, gn_bias)[1]
    activated = jax.nn.silu(shifted)
    spatial = spatial_sweep(jnp.pad(activated, ((0, 0), (1, 1), (0, 0), (1, 1))), w_spatial)
    hidden = latent + temporal_sweep(jnp.pad(spatial, ((1, 1), (0, 0), (0, 0), (0, 0))), w_temporal)
    normed = layer_stats(hidden, ln_gain, ln_bias)[0]
    attended = attend(mix(normed, w_query), mix(normed, w_key), mix(normed, w_value))[0]
    return hidden + mix(attended, w_out)

def reference(latent, cotangent, gn_gain, gn_bias, w_spatial, w_temporal, ln_gain, ln_bias, w_query, w_key, w_value, w_out):

    def forward(inputs):
        return block(inputs, gn_gain, gn_bias, w_spatial, w_temporal, ln_gain, ln_bias, w_query, w_key, w_value, w_out)
    output, pullback = jax.vjp(forward, latent)
    grad_latent = pullback(cotangent)[0]
    return (output, grad_latent)
```

```python
import functools

import jax
import jax.numpy as jnp
from jax import lax
from jax.experimental import pallas as pl
from jax.experimental.pallas import tpu as pltpu
from jax.sharding import PartitionSpec as P

C = 320
GROUPS = 32
PER_GROUP = C // GROUPS
HEADS = 5
HEAD_DIM = 64
EPSILON = 1e-05
LANES = 128
KDIM = 1024
QUARTER = C // 4
F32 = jnp.float32
BF16 = jnp.bfloat16
HIGHEST = lax.Precision.HIGHEST
MESH = pl.DeviceIdType.MESH
NT = (((1,), (1,)), ((), ()))

LAT, COT, SPA, GSP, GHI, OUT = 0, 2, 4, 6, 8, 10


def iota(shape, dim):
    return lax.broadcasted_iota(jnp.int32, shape, dim)


def roll(x, shift):
    shift = shift % x.shape[1]
    return x if shift == 0 else pltpu.roll(x, shift, 1)


def dot(a, b):
    return jnp.dot(a, b, preferred_element_type=F32)


def dot_nt(a, b):
    return lax.dot_general(a, b, NT, preferred_element_type=F32)


def exact_nt(a, b):
    return lax.dot_general(a, b, NT, precision=HIGHEST, preferred_element_type=F32)


def split(x):
    hi = x.astype(BF16)
    lo = (x - hi.astype(F32)).astype(BF16)
    return hi, lo


def transpose_chunks(xs):
    lane = iota(xs[0].shape, 1)
    bits = [(lane & (16 << i)) != 0 for i in range(3)]
    ys = [roll(x, 16 * m) for m, x in enumerate(xs)]
    out = []
    for j in range(8):
        level = [ys[(p - j) % 8] for p in range(8)]
        for bit in bits:
            level = [
                jnp.where(bit, level[2 * i + 1], level[2 * i]) for i in range(len(level) // 2)
            ]
        out.append(roll(level[0], -16 * j))
    return out


def interleave(x0, x1):
    low = (iota(x0.shape, 1) & 8) == 0
    return jnp.where(low, x0, roll(x1, 8)), jnp.where(low, roll(x0, -8), x1)


def put3(ref, base, lanes, x):
    hi, lo = split(x)
    ref[pl.ds(base, 256), lanes] = hi[:256]
    ref[pl.ds(base + 256, 256), lanes] = lo[:256]
    ref[pl.ds(base + 512, 256), lanes] = hi[:256]
    ref[pl.ds(base + 768, 64), lanes] = hi[256:]
    ref[pl.ds(base + 832, 64), lanes] = lo[256:]
    ref[pl.ds(base + 896, 64), lanes] = hi[256:]


def prepare(w, ref):
    hi = w.astype(BF16).astype(F32)
    lo = w - hi
    ref[:, 0:256] = hi[:, :256].astype(BF16)
    ref[:, 256:512] = hi[:, :256].astype(BF16)
    ref[:, 512:768] = lo[:, :256].astype(BF16)
    ref[:, 768:896] = jnp.concatenate([hi[:, 256:], hi[:, 256:]], axis=1).astype(BF16)
    ref[:, 896:1024] = jnp.concatenate([lo[:, 256:], jnp.zeros((C, 64), F32)], axis=1).astype(BF16)


def kernel(
    n_frame,
    n_row,
    latent,
    cotangent,
    vecs,
    w_spatial,
    w_temporal,
    w_query,
    w_key,
    w_value,
    w_out,
    output,
    grad_latent,
    lat4,
    cot_own,
    gs4,
    hat_s,
    fac_s,
    ghid,
    gact,
    wsp,
    wte,
    wat,
    lsp,
    lte_f,
    lte_b,
    lqkv,
    lat_b,
    lout_f,
    rhs9,
    rhs3,
    rhs1,
    sbuf,
    rbuf,
    stat_s,
    stat_r,
    bcast,
    lcol,
    scol,
    qkv,
    gcol,
    acol,
    hcol,
    dqkv,
    load_sem,
    ssem,
    rsem,
    halo_s,
    halo_r,
    stat_ss,
    stat_rs,
):
    fi = lax.axis_index("frame")
    ri = lax.axis_index("row")
    members = 2 * n_row * PER_GROUP * LANES
    has_low = ri > 0
    has_high = ri < n_row - 1

    loads = []
    for r in range(2):
        for f in range(2):
            loads.append((latent.at[f, r], lat4.at[1 + r, f]))
    for r in range(2):
        for f in range(2):
            loads.append((cotangent.at[f, r], cot_own.at[r, f]))
    loads.append((w_spatial, wsp))
    loads.append((w_temporal, wte))
    for i, w in enumerate((w_query, w_key, w_value, w_out)):
        loads.append((w, wat.at[i]))
    copies = [
        pltpu.make_async_copy(src, dst, load_sem.at[i]) for i, (src, dst) in enumerate(loads)
    ]
    for c in copies:
        c.start()

    barrier = pltpu.get_barrier_semaphore()

    @pl.loop(1, n_row)
    def _(k):
        pl.semaphore_signal(
            barrier, inc=1, device_id={"row": lax.rem(ri + k, n_row)}, device_id_type=MESH
        )

    @pl.loop(1, n_frame)
    def _(k):
        pl.semaphore_signal(
            barrier, inc=1, device_id={"frame": lax.rem(fi + k, n_frame)}, device_id_type=MESH
        )

    def a2a_send(t):
        @pl.loop(1, n_frame)
        def _(k):
            dest = lax.rem(fi + k, n_frame)
            pltpu.make_async_remote_copy(
                src_ref=sbuf.at[t, dest],
                dst_ref=rbuf.at[t, fi],
                send_sem=ssem.at[t],
                recv_sem=rsem.at[t],
                device_id={"frame": dest},
                device_id_type=MESH,
            ).start()

        rbuf[t, fi] = sbuf[t, fi]

    def bytes_wait(ref, sem):
        pltpu.make_async_copy(ref, ref, sem).wait()

    def a2a_wait(t):
        bytes_wait(rbuf.at[t, pl.ds(0, n_frame - 1)], rsem.at[t])

    def pack_frame(src, t):
        @pl.loop(0, 5)
        def _(i):
            xs = []
            for q in range(4):
                start = pl.multiple_of(q * QUARTER + i * 16, 16)
                xs.extend(interleave(src(0, start), src(1, start)))
            for j, x in enumerate(transpose_chunks(xs)):
                sbuf[t, j, pl.ds(pl.multiple_of(i * 16, 16), 16), :] = x

    def unpack_frame(t, store):
        @pl.loop(0, 5)
        def _(i):
            at = pl.ds(pl.multiple_of(i * 16, 16), 16)
            ys = transpose_chunks([rbuf[t, j, at, :] for j in range(8)])
            for q in range(4):
                x0, x1 = interleave(ys[2 * q], ys[2 * q + 1])
                start = pl.multiple_of(q * QUARTER + i * 16, 16)
                store(0, start, x0)
                store(1, start, x1)

    def pack_col(src, t):
        @pl.loop(0, 5)
        def _(i):
            xs = []
            for q in range(4):
                start = pl.multiple_of(q * QUARTER + i * 16, 16)
                for h in range(2):
                    xs.append(src[pl.ds(start, 16), h * LANES : (h + 1) * LANES])
            for s, x in enumerate(transpose_chunks(xs)):
                sbuf[t, s, pl.ds(pl.multiple_of(i * 16, 16), 16), :] = x

    def unpack_col(t, dst):
        @pl.loop(0, 5)
        def _(i):
            at = pl.ds(pl.multiple_of(i * 16, 16), 16)
            ys = transpose_chunks([rbuf[t, s, at, :] for s in range(8)])
            for q in range(4):
                start = pl.multiple_of(q * QUARTER + i * 16, 16)
                for h in range(2):
                    dst[pl.ds(start, 16), h * LANES : (h + 1) * LANES] = ys[2 * q + h]

    chan = iota((C, LANES), 0)
    group = iota((C, LANES), 1)
    member = ((chan >= group * PER_GROUP) & (chan < group * PER_GROUP + PER_GROUP)).astype(F32)

    def pack_stats(which, parts):
        total = jnp.zeros((8, C), F32)
        at = iota((8, LANES), 0)
        for k, part in enumerate(parts):
            total = total + exact_nt((at == k).astype(F32), part)
        tile = jnp.dot(total, member, precision=HIGHEST, preferred_element_type=F32)
        stat_s[which] = tile
        stat_r[which, ri] = tile

    def send_stats(which):
        @pl.loop(1, n_row)
        def _(k):
            pltpu.make_async_remote_copy(
                src_ref=stat_s.at[which],
                dst_ref=stat_r.at[which, ri],
                send_sem=stat_ss.at[which],
                recv_sem=stat_rs.at[which],
                device_id={"row": lax.rem(ri + k, n_row)},
                device_id_type=MESH,
            ).start()

    def total_stats(which):
        bytes_wait(stat_r.at[which, pl.ds(0, n_row - 1)], stat_rs.at[which])
        return jnp.sum(stat_r[which], axis=0) * (1.0 / members)

    def spread(rows, at):
        cols = exact_nt(member, rows)
        for k in range(4):
            bcast[at + k] = jnp.broadcast_to(cols[:, k : k + 1], (C, LANES))

    def halo_copies(buf, which):
        up = pltpu.make_async_remote_copy(
            src_ref=buf.at[2],
            dst_ref=buf.at[0],
            send_sem=halo_s.at[which],
            recv_sem=halo_r.at[which],
            device_id={"row": lax.rem(ri + 1, n_row)},
            device_id_type=MESH,
        )
        down = pltpu.make_async_remote_copy(
            src_ref=buf.at[1],
            dst_ref=buf.at[3],
            send_sem=halo_s.at[which + 1],
            recv_sem=halo_r.at[which + 1],
            device_id={"row": lax.rem(ri + n_row - 1, n_row)},
            device_id_type=MESH,
        )
        return up, down

    for c in copies[:4]:
        c.wait()
    parts = []
    for f in range(2):
        a, b = lat4[1, f], lat4[2, f]
        parts.append(a + b)
    for f in range(2):
        a, b = lat4[1, f], lat4[2, f]
        parts.append(a * a + b * b)
    pack_stats(0, parts)
    for r in range(2):
        pack_frame(lambda f, start: lat4[1 + r, f, pl.ds(start, 16), :], LAT + r)
    for c in copies[4:8]:
        c.wait()
    for r in range(2):
        pack_frame(lambda f, start: cot_own[r, f, pl.ds(start, 16), :], COT + r)

    pl.semaphore_wait(barrier, n_row - 1 + n_frame - 1)
    send_stats(0)
    lat_up, lat_down = halo_copies(lat4, 0)
    lat_up.start()
    lat_down.start()
    a2a_send(LAT)
    a2a_send(COT)

    for c in copies[8:]:
        c.wait()

    @pl.loop(0, 9)
    def _(t):
        prepare(wsp[t].T, lsp.at[t])

    @pl.loop(0, 3)
    def _(t):
        prepare(wte[t].T, lte_f.at[t])

    @pl.loop(0, 12)
    def _(t):
        rhs9[pl.ds(pl.multiple_of(t * KDIM + 960, 64), 64), :] = jnp.zeros((64, 256), BF16)

    for t in range(3):
        rhs3[t, pl.ds(960, 64), :] = jnp.zeros((64, 256), BF16)
    rhs1[pl.ds(960, 64), :] = jnp.zeros((64, 256), BF16)

    eye = (iota((C, C), 0) == iota((C, C), 1)).astype(F32)
    cols = exact_nt(eye, vecs[...])
    for k in range(4):
        bcast[4 + k] = jnp.broadcast_to(cols[:, k : k + 1], (C, LANES))

    mean2 = total_stats(0)
    at8 = iota((8, LANES), 0)
    var = pltpu.roll(mean2, 6, 0) - mean2 * mean2
    rstd = lax.rsqrt(jnp.where(at8 < 2, var, 1.0) + EPSILON)
    spread(jnp.where(at8 < 2, mean2, pltpu.roll(rstd, 2, 0)), 0)

    lat_up.wait_recv()
    lat_down.wait_recv()

    lane = iota((C, LANES), 1)

    def shifted_rhs(r4, f, x):
        for b in range(3):
            if b == 0:
                y = jnp.where(lane == 0, 0.0, roll(x, 1))
            elif b == 1:
                y = x
            else:
                y = jnp.where(lane == LANES - 1, 0.0, roll(x, LANES - 1))
            base = pl.multiple_of((r4 * 3 + b) * KDIM, KDIM)
            put3(rhs9, base, pl.ds(f * LANES, LANES), y)

    def inside(r4):
        return ((r4 > 0) | has_low) & ((r4 < 3) | has_high)

    @pl.loop(0, 4)
    def _(r4):
        for f in range(2):
            hat = (lat4[r4, f] - bcast[f]) * bcast[2 + f]
            shifted = hat * bcast[4] + bcast[5]
            sigma = 1.0 / (1.0 + jnp.exp(-shifted))
            act = shifted * sigma
            hat_s[r4, f] = hat
            fac_s[r4, f] = sigma * (1.0 + shifted * (1.0 - sigma)) * bcast[4]
            shifted_rhs(r4, f, jnp.where(inside(r4), act, 0.0))

    def conv(rows, taps, base):
        total = None
        for t in taps:
            start = pl.multiple_of(base + (t - taps[0]) * KDIM, KDIM)
            term = dot(lsp[t], rhs9[pl.ds(start, KDIM), :])
            total = term if total is None else total + term
        return total

    @pl.loop(0, 2)
    def _(r):
        scol[...] = conv(r, list(range(9)), r * (3 * KDIM))
        pack_frame(
            lambda f, start: scol[pl.ds(start, 16), f * LANES : (f + 1) * LANES], SPA + r
        )
        a2a_send(SPA + r)

        @pl.when(r == 0)
        def _():
            a2a_send(LAT + 1)

    a2a_send(COT + 1)

    for i in range(3):
        prepare(wat[i].T, lqkv.at[pl.ds(i * C, C)])
    for i in range(4):
        prepare(wat[i], lat_b.at[i])
    prepare(wat[3].T, lout_f)
    for k in range(3):
        prepare(wte[2 - k], lte_b.at[k])

    half = LANES
    same = (iota((half, half), 0) & 7) == (iota((half, half), 1) & 7)
    scale = HEAD_DIM ** (-0.5)

    def temporal(x, h):
        lanes = pl.ds(h * half, half)
        put3(rhs3.at[0], 0, lanes, jnp.where(lane < 8, 0.0, roll(x, 8)))
        put3(rhs3.at[1], 0, lanes, x)
        put3(rhs3.at[2], 0, lanes, jnp.where(lane >= half - 8, 0.0, roll(x, half - 8)))

    def temporal_mix(weights):
        return (
            dot(weights[0], rhs3[0]) + dot(weights[1], rhs3[1]) + dot(weights[2], rhs3[2])
        )

    def twice(k):
        return jnp.concatenate([bcast[k], bcast[k]], axis=1)

    def stack3(x, axis):
        hi, lo = split(x)
        return jnp.concatenate([hi, lo, hi], axis=axis)

    def weigh3(x, axis):
        hi, lo = split(x)
        return jnp.concatenate([hi, hi, lo], axis=axis)

    def turned(x):
        hi = x.astype(BF16).astype(F32)
        lo = x - hi
        return jnp.concatenate([hi, hi, lo], axis=0).T.astype(BF16)

    @pl.loop(0, 2)
    def _(r):
        a2a_wait(LAT + r)
        unpack_col(LAT + r, lcol)
        a2a_wait(SPA + r)
        unpack_col(SPA + r, scol)
        for h in range(2):
            temporal(scol[:, h * half : (h + 1) * half], h)
        hidden = lcol[...] + temporal_mix(lte_f)
        hcol[r] = hidden
        centered = hidden - jnp.sum(hidden, axis=0, keepdims=True) * (1.0 / C)
        spread_ = jnp.sum(centered * centered, axis=0, keepdims=True) * (1.0 / C)
        ln_rstd = lax.rsqrt(spread_ + EPSILON)
        normal = centered * ln_rstd
        lcol[...] = normal
        normed = normal * twice(6) + twice(7)
        for h in range(2):
            put3(rhs1, 0, pl.ds(h * half, half), normed[:, h * half : (h + 1) * half])
        qkv[...] = dot(lqkv[...], rhs1[...])

        a2a_wait(COT + r)
        unpack_col(COT + r, gcol)
        for h in range(2):
            put3(rhs1, 0, pl.ds(h * half, half), gcol[:, h * half : (h + 1) * half])
        scol[...] = dot(lat_b[3], rhs1[...])

        for head in range(HEADS):
            for h in range(2):
                rows = slice(head * HEAD_DIM, (head + 1) * HEAD_DIM)
                lanes = slice(h * half, (h + 1) * half)
                q = qkv[rows, lanes]
                k = qkv[C + head * HEAD_DIM : C + (head + 1) * HEAD_DIM, lanes]
                v = qkv[2 * C + head * HEAD_DIM : 2 * C + (head + 1) * HEAD_DIM, lanes]
                g = scol[rows, lanes]
                scores = jnp.where(same, dot(turned(k), stack3(q, 0)) * scale, -1e30)
                e = jnp.exp(scores - jnp.max(scores, axis=0, keepdims=True))
                p = e * (1.0 / jnp.sum(e, axis=0, keepdims=True))
                p3 = stack3(p, 0)
                acol[r, rows, lanes] = dot(weigh3(v, 1), p3)
                gp = dot(turned(v), stack3(g, 0))
                gs = p * (gp - jnp.sum(p * gp, axis=0, keepdims=True)) * scale
                dqkv[0, rows, lanes] = dot(weigh3(k, 1), stack3(gs, 0))
                dqkv[1, rows, lanes] = dot_nt(weigh3(q, 1), stack3(gs, 1))
                dqkv[2, rows, lanes] = dot_nt(weigh3(g, 1), stack3(p, 1))

        for i in range(3):
            for h in range(2):
                put3(
                    rhs3.at[i], 0, pl.ds(h * half, half), dqkv[i, :, h * half : (h + 1) * half]
                )
        scaled = temporal_mix(lat_b) * twice(6)
        normal = lcol[...]
        first = jnp.sum(scaled, axis=0, keepdims=True) * (1.0 / C)
        second = jnp.sum(scaled * normal, axis=0, keepdims=True) * (1.0 / C)
        gcol[...] = gcol[...] + ln_rstd * (scaled - first - normal * second)
        for h in range(2):
            temporal(gcol[:, h * half : (h + 1) * half], h)
        scol[...] = temporal_mix(lte_b)
        pack_col(scol, GSP + r)
        a2a_send(GSP + r)
        pack_col(gcol, GHI + r)

    a2a_send(GHI)
    a2a_send(GHI + 1)

    @pl.loop(0, 2)
    def _(r):
        for h in range(2):
            put3(rhs1, 0, pl.ds(h * half, half), acol[r, :, h * half : (h + 1) * half])
        scol[...] = hcol[r] + dot(lout_f[...], rhs1[...])
        pack_col(scol, OUT + r)
        a2a_send(OUT + r)

    @pl.loop(0, 9)
    def _(t):
        prepare(wsp[8 - t], lsp.at[t])

    gs_up, gs_down = halo_copies(gs4, 2)

    def store_gs(r):
        def store(f, start, x):
            gs4[1 + r, f, pl.ds(start, 16), :] = x

        return store

    a2a_wait(GSP)
    unpack_frame(GSP, store_gs(0))
    gs_down.start()
    a2a_wait(GSP + 1)
    unpack_frame(GSP + 1, store_gs(1))
    gs_up.start()

    @pl.loop(1, 3)
    def _(r4):
        for f in range(2):
            shifted_rhs(r4, f, gs4[r4, f])

    gact[0] = conv(0, list(range(3, 9)), 3 * KDIM)
    gact[1] = conv(1, list(range(0, 6)), 3 * KDIM)

    def store_hid(r):
        def store(f, start, x):
            ghid[r, f, pl.ds(start, 16), :] = x

        return store

    def store_out(r):
        def store(f, start, x):
            output[f, r, pl.ds(start, 16), :] = x

        return store

    for r in range(2):
        a2a_wait(GHI + r)
        unpack_frame(GHI + r, store_hid(r))

    gs_up.wait_recv()
    gs_down.wait_recv()
    for r4 in (0, 3):
        for f in range(2):
            shifted_rhs(r4, f, jnp.where(inside(r4), gs4[r4, f], 0.0))
    gact[0] = gact[0] + conv(0, list(range(0, 3)), 0)
    gact[1] = gact[1] + conv(1, list(range(6, 9)), 9 * KDIM)

    parts = []
    for f in range(2):
        lanes = slice(f * LANES, (f + 1) * LANES)
        a = gact[0, :, lanes] * fac_s[1, f]
        b = gact[1, :, lanes] * fac_s[2, f]
        gact[0, :, lanes] = a
        gact[1, :, lanes] = b
        parts.append((a + b, a * hat_s[1, f] + b * hat_s[2, f]))
    pack_stats(1, [parts[0][0], parts[1][0], parts[0][1], parts[1][1]])
    send_stats(1)

    for r in range(2):
        a2a_wait(OUT + r)
        unpack_frame(OUT + r, store_out(r))

    spread(total_stats(1), 4)
    for r in range(2):
        for f in range(2):
            grad_latent[f, r] = ghid[r, f] + bcast[2 + f] * (
                gact[r, :, f * LANES : (f + 1) * LANES]
                - bcast[4 + f]
                - hat_s[1 + r, f] * bcast[6 + f]
            )

    for t in range(12):
        bytes_wait(sbuf.at[t, pl.ds(0, n_frame - 1)], ssem.at[t])
    for copy in (lat_up, lat_down, gs_up, gs_down):
        copy.wait_send()
    for which in range(2):
        bytes_wait(stat_r.at[which, pl.ds(0, n_row - 1)], stat_ss.at[which])


def per_device(
    n_frame,
    n_row,
    latent,
    cotangent,
    gn_gain,
    gn_bias,
    w_spatial,
    w_temporal,
    ln_gain,
    ln_bias,
    w_query,
    w_key,
    w_value,
    w_out,
):
    frames, rows, chans, cols = latent.shape
    vecs = jnp.concatenate(
        [jnp.stack([gn_gain, gn_bias, ln_gain, ln_bias]), jnp.zeros((4, chans), F32)]
    )
    anywhere = pl.BlockSpec(memory_space=pl.ANY)
    inside = pl.BlockSpec(memory_space=pltpu.VMEM)
    vm = pltpu.VMEM
    dma = pltpu.SemaphoreType.DMA
    return pl.pallas_call(
        functools.partial(kernel, n_frame, n_row),
        out_shape=(
            jax.ShapeDtypeStruct(latent.shape, F32),
            jax.ShapeDtypeStruct(latent.shape, F32),
        ),
        in_specs=[anywhere, anywhere, inside] + [anywhere] * 6,
        out_specs=(inside, inside),
        scratch_shapes=[
            vm((4, 2, C, LANES), F32),
            vm((2, 2, C, LANES), F32),
            vm((4, 2, C, LANES), F32),
            vm((4, 2, C, LANES), F32),
            vm((4, 2, C, LANES), F32),
            vm((2, 2, C, LANES), F32),
            vm((2, C, 256), F32),
            vm((9, C, C), F32),
            vm((3, C, C), F32),
            vm((4, C, C), F32),
            vm((9, C, KDIM), BF16),
            vm((3, C, KDIM), BF16),
            vm((3, C, KDIM), BF16),
            vm((3 * C, KDIM), BF16),
            vm((4, C, KDIM), BF16),
            vm((C, KDIM), BF16),
            vm((12 * KDIM, 256), BF16),
            vm((3, KDIM, 256), BF16),
            vm((KDIM, 256), BF16),
            vm((12, 8, QUARTER, LANES), F32),
            vm((12, 8, QUARTER, LANES), F32),
            vm((2, 8, LANES), F32),
            vm((2, n_row, 8, LANES), F32),
            vm((8, C, LANES), F32),
            vm((C, 256), F32),
            vm((C, 256), F32),
            vm((3 * C, 256), F32),
            vm((C, 256), F32),
            vm((2, C, 256), F32),
            vm((2, C, 256), F32),
            vm((3, C, 256), F32),
            dma((14,)),
            dma((12,)),
            dma((12,)),
            dma((4,)),
            dma((4,)),
            dma((2,)),
            dma((2,)),
        ],
        compiler_params=pltpu.CompilerParams(
            collective_id=0, has_side_effects=True, vmem_limit_bytes=62 * 1024 * 1024
        ),
        cost_estimate=pl.CostEstimate(flops=10**10, bytes_accessed=10**7, transcendentals=10**6),
    )(
        latent,
        cotangent,
        vecs,
        w_spatial.reshape(9, C, C),
        w_temporal,
        w_query,
        w_key,
        w_value,
        w_out,
    )


def solution(mesh):
    sizes = dict(mesh.shape)
    return jax.shard_map(
        functools.partial(per_device, sizes["frame"], sizes["row"]),
        mesh=mesh,
        in_specs=(P("frame", "row", None, None), P("frame", "row", None, None))
        + (P(),) * 10,
        out_specs=(P("frame", "row", None, None), P("frame", "row", None, None)),
        check_vma=False,
    )
```

```python
import functools

import jax
import jax.numpy as jnp
from jax import lax
from jax.experimental import pallas as pl
from jax.experimental.pallas import tpu as pltpu
from jax.sharding import PartitionSpec as P

C = 320
GROUPS = 32
PER_GROUP = C // GROUPS
HEADS = 5
HEAD_DIM = 64
EPSILON = 1e-05
LANES = 128
KDIM = 1024
QUARTER = C // 4
F32 = jnp.float32
BF16 = jnp.bfloat16
HIGHEST = lax.Precision.HIGHEST
MESH = pl.DeviceIdType.MESH
NT = (((1,), (1,)), ((), ()))

LAT, COT, SPA, GSP, GHI, OUT = 0, 2, 4, 6, 8, 10


def iota(shape, dim):
    return lax.broadcasted_iota(jnp.int32, shape, dim)


def roll(x, shift):
    shift = shift % x.shape[1]
    return x if shift == 0 else pltpu.roll(x, shift, 1)


def dot(a, b):
    return jnp.dot(a, b, preferred_element_type=F32)


def dot_nt(a, b):
    return lax.dot_general(a, b, NT, preferred_element_type=F32)


def exact_nt(a, b):
    return lax.dot_general(a, b, NT, precision=HIGHEST, preferred_element_type=F32)


def split(x):
    hi = x.astype(BF16)
    lo = (x - hi.astype(F32)).astype(BF16)
    return hi, lo


def transpose_chunks(xs):
    lane = iota(xs[0].shape, 1)
    bits = [(lane & (16 << i)) != 0 for i in range(3)]
    ys = [roll(x, 16 * m) for m, x in enumerate(xs)]
    out = []
    for j in range(8):
        level = [ys[(p - j) % 8] for p in range(8)]
        for bit in bits:
            level = [
                jnp.where(bit, level[2 * i + 1], level[2 * i]) for i in range(len(level) // 2)
            ]
        out.append(roll(level[0], -16 * j))
    return out


def interleave(x0, x1):
    low = (iota(x0.shape, 1) & 8) == 0
    return jnp.where(low, x0, roll(x1, 8)), jnp.where(low, roll(x0, -8), x1)


def put3(ref, base, lanes, x):
    hi, lo = split(x)
    ref[pl.ds(base, 256), lanes] = hi[:256]
    ref[pl.ds(base + 256, 256), lanes] = lo[:256]
    ref[pl.ds(base + 512, 256), lanes] = hi[:256]
    ref[pl.ds(base + 768, 64), lanes] = hi[256:]
    ref[pl.ds(base + 832, 64), lanes] = lo[256:]
    ref[pl.ds(base + 896, 64), lanes] = hi[256:]


def prepare(w, ref):
    hi = w.astype(BF16).astype(F32)
    lo = w - hi
    ref[:, 0:256] = hi[:, :256].astype(BF16)
    ref[:, 256:512] = hi[:, :256].astype(BF16)
    ref[:, 512:768] = lo[:, :256].astype(BF16)
    ref[:, 768:896] = jnp.concatenate([hi[:, 256:], hi[:, 256:]], axis=1).astype(BF16)
    ref[:, 896:1024] = jnp.concatenate([lo[:, 256:], jnp.zeros((C, 64), F32)], axis=1).astype(BF16)


def kernel(
    n_frame,
    n_row,
    latent,
    cotangent,
    vec0,
    vec1,
    vec2,
    vec3,
    w_spatial,
    w_temporal,
    w_query,
    w_key,
    w_value,
    w_out,
    result,
    lat4,
    cot_own,
    gs4,
    hat_s,
    fac_s,
    ghid,
    gact,
    wsp,
    wte,
    wat,
    lsp,
    lte_f,
    lte_b,
    lqkv,
    lat_b,
    lout_f,
    rhs9,
    rhs3,
    rhs1,
    sbuf,
    rbuf,
    stat_s,
    stat_r,
    bcast,
    lcol,
    scol,
    qkv,
    gcol,
    acol,
    hcol,
    dqkv,
    load_sem,
    ssem,
    rsem,
    halo_s,
    halo_r,
    stat_ss,
    stat_rs,
):
    fi = lax.axis_index("frame")
    ri = lax.axis_index("row")
    members = 2 * n_row * PER_GROUP * LANES
    has_low = ri > 0
    has_high = ri < n_row - 1

    output, grad_latent = result.at[0], result.at[1]
    loads = []
    for r in range(2):
        for f in range(2):
            loads.append((latent.at[f, r], lat4.at[1 + r, f]))
    for r in range(2):
        for f in range(2):
            loads.append((cotangent.at[f, r], cot_own.at[r, f]))
    loads.append((w_spatial, wsp))
    loads.append((w_temporal, wte))
    for i, w in enumerate((w_query, w_key, w_value, w_out)):
        loads.append((w, wat.at[i]))
    copies = [
        pltpu.make_async_copy(src, dst, load_sem.at[i]) for i, (src, dst) in enumerate(loads)
    ]
    for c in copies:
        c.start()

    barrier = pltpu.get_barrier_semaphore()

    @pl.loop(1, n_row)
    def _(k):
        pl.semaphore_signal(
            barrier, inc=1, device_id={"row": lax.rem(ri + k, n_row)}, device_id_type=MESH
        )

    @pl.loop(1, n_frame)
    def _(k):
        pl.semaphore_signal(
            barrier, inc=1, device_id={"frame": lax.rem(fi + k, n_frame)}, device_id_type=MESH
        )

    def a2a_send(t):
        @pl.loop(1, n_frame)
        def _(k):
            dest = lax.rem(fi + k, n_frame)
            pltpu.make_async_remote_copy(
                src_ref=sbuf.at[t, dest],
                dst_ref=rbuf.at[t, fi],
                send_sem=ssem.at[t],
                recv_sem=rsem.at[t],
                device_id={"frame": dest},
                device_id_type=MESH,
            ).start()

        rbuf[t, fi] = sbuf[t, fi]

    def bytes_wait(ref, sem):
        pltpu.make_async_copy(ref, ref, sem).wait()

    def a2a_wait(t):
        bytes_wait(rbuf.at[t, pl.ds(0, n_frame - 1)], rsem.at[t])

    def pack_frame(src, t):
        @pl.loop(0, 5, unroll=5)
        def _(i):
            xs = []
            for q in range(4):
                start = pl.multiple_of(q * QUARTER + i * 16, 16)
                xs.extend(interleave(src(0, start), src(1, start)))
            for j, x in enumerate(transpose_chunks(xs)):
                sbuf[t, j, pl.ds(pl.multiple_of(i * 16, 16), 16), :] = x

    def unpack_frame(t, store):
        @pl.loop(0, 5, unroll=5)
        def _(i):
            at = pl.ds(pl.multiple_of(i * 16, 16), 16)
            ys = transpose_chunks([rbuf[t, j, at, :] for j in range(8)])
            for q in range(4):
                x0, x1 = interleave(ys[2 * q], ys[2 * q + 1])
                start = pl.multiple_of(q * QUARTER + i * 16, 16)
                store(0, start, x0)
                store(1, start, x1)

    def pack_col(src, t):
        @pl.loop(0, 5, unroll=5)
        def _(i):
            xs = []
            for q in range(4):
                start = pl.multiple_of(q * QUARTER + i * 16, 16)
                for h in range(2):
                    xs.append(src[pl.ds(start, 16), h * LANES : (h + 1) * LANES])
            for s, x in enumerate(transpose_chunks(xs)):
                sbuf[t, s, pl.ds(pl.multiple_of(i * 16, 16), 16), :] = x

    def unpack_col(t, dst):
        @pl.loop(0, 5, unroll=5)
        def _(i):
            at = pl.ds(pl.multiple_of(i * 16, 16), 16)
            ys = transpose_chunks([rbuf[t, s, at, :] for s in range(8)])
            for q in range(4):
                start = pl.multiple_of(q * QUARTER + i * 16, 16)
                for h in range(2):
                    dst[pl.ds(start, 16), h * LANES : (h + 1) * LANES] = ys[2 * q + h]

    chan = iota((C, LANES), 0)
    group = iota((C, LANES), 1)
    member = ((chan >= group * PER_GROUP) & (chan < group * PER_GROUP + PER_GROUP)).astype(F32)

    def pack_stats(which, parts):
        total = jnp.zeros((8, C), F32)
        at = iota((8, LANES), 0)
        for k, part in enumerate(parts):
            total = total + exact_nt((at == k).astype(F32), part)
        tile = jnp.dot(total, member, precision=HIGHEST, preferred_element_type=F32)
        stat_s[which] = tile
        stat_r[which, ri] = tile

    def send_stats(which):
        @pl.loop(1, n_row)
        def _(k):
            pltpu.make_async_remote_copy(
                src_ref=stat_s.at[which],
                dst_ref=stat_r.at[which, ri],
                send_sem=stat_ss.at[which],
                recv_sem=stat_rs.at[which],
                device_id={"row": lax.rem(ri + k, n_row)},
                device_id_type=MESH,
            ).start()

    def total_stats(which):
        bytes_wait(stat_r.at[which, pl.ds(0, n_row - 1)], stat_rs.at[which])
        return jnp.sum(stat_r[which], axis=0) * (1.0 / members)

    def spread(rows, at):
        cols = exact_nt(member, rows)
        for k in range(4):
            bcast[at + k] = jnp.broadcast_to(cols[:, k : k + 1], (C, LANES))

    def halo_copies(buf, which):
        up = pltpu.make_async_remote_copy(
            src_ref=buf.at[2],
            dst_ref=buf.at[0],
            send_sem=halo_s.at[which],
            recv_sem=halo_r.at[which],
            device_id={"row": lax.rem(ri + 1, n_row)},
            device_id_type=MESH,
        )
        down = pltpu.make_async_remote_copy(
            src_ref=buf.at[1],
            dst_ref=buf.at[3],
            send_sem=halo_s.at[which + 1],
            recv_sem=halo_r.at[which + 1],
            device_id={"row": lax.rem(ri + n_row - 1, n_row)},
            device_id_type=MESH,
        )
        return up, down

    for c in copies[:4]:
        c.wait()
    parts = []
    for f in range(2):
        a, b = lat4[1, f], lat4[2, f]
        parts.append(a + b)
    for f in range(2):
        a, b = lat4[1, f], lat4[2, f]
        parts.append(a * a + b * b)
    pack_stats(0, parts)
    for r in range(2):
        pack_frame(lambda f, start: lat4[1 + r, f, pl.ds(start, 16), :], LAT + r)
    for c in copies[4:8]:
        c.wait()
    for r in range(2):
        pack_frame(lambda f, start: cot_own[r, f, pl.ds(start, 16), :], COT + r)

    pl.semaphore_wait(barrier, n_row - 1 + n_frame - 1)
    send_stats(0)
    lat_up, lat_down = halo_copies(lat4, 0)
    lat_up.start()
    lat_down.start()
    a2a_send(LAT)
    a2a_send(COT)

    for c in copies[8:]:
        c.wait()

    @pl.loop(0, 9)
    def _(t):
        prepare(wsp[t].T, lsp.at[t])

    @pl.loop(0, 3)
    def _(t):
        prepare(wte[t].T, lte_f.at[t])

    @pl.loop(0, 12)
    def _(t):
        rhs9[pl.ds(pl.multiple_of(t * KDIM + 960, 64), 64), :] = jnp.zeros((64, 256), BF16)

    for t in range(3):
        rhs3[t, pl.ds(960, 64), :] = jnp.zeros((64, 256), BF16)
    rhs1[pl.ds(960, 64), :] = jnp.zeros((64, 256), BF16)

    eye = (iota((C, C), 0) == iota((C, C), 1)).astype(F32)
    vecs = [v[...].reshape(1, C) for v in (vec0, vec1, vec2, vec3)] + [jnp.zeros((4, C), F32)]
    cols = exact_nt(eye, jnp.concatenate(vecs, axis=0))
    for k in range(4):
        bcast[4 + k] = jnp.broadcast_to(cols[:, k : k + 1], (C, LANES))

    mean2 = total_stats(0)
    at8 = iota((8, LANES), 0)
    var = pltpu.roll(mean2, 6, 0) - mean2 * mean2
    rstd = lax.rsqrt(jnp.where(at8 < 2, var, 1.0) + EPSILON)
    spread(jnp.where(at8 < 2, mean2, pltpu.roll(rstd, 2, 0)), 0)

    lat_up.wait_recv()
    lat_down.wait_recv()

    lane = iota((C, LANES), 1)

    def shifted_rhs(r4, f, x):
        for b in range(3):
            if b == 0:
                y = jnp.where(lane == 0, 0.0, roll(x, 1))
            elif b == 1:
                y = x
            else:
                y = jnp.where(lane == LANES - 1, 0.0, roll(x, LANES - 1))
            base = pl.multiple_of((r4 * 3 + b) * KDIM, KDIM)
            put3(rhs9, base, pl.ds(f * LANES, LANES), y)

    def inside(r4):
        return ((r4 > 0) | has_low) & ((r4 < 3) | has_high)

    @pl.loop(0, 4)
    def _(r4):
        for f in range(2):
            hat = (lat4[r4, f] - bcast[f]) * bcast[2 + f]
            shifted = hat * bcast[4] + bcast[5]
            sigma = 1.0 / (1.0 + jnp.exp(-shifted))
            act = shifted * sigma
            hat_s[r4, f] = hat
            fac_s[r4, f] = sigma * (1.0 + shifted * (1.0 - sigma)) * bcast[4]
            shifted_rhs(r4, f, jnp.where(inside(r4), act, 0.0))

    def conv(rows, taps, base):
        total = None
        for t in taps:
            start = pl.multiple_of(base + (t - taps[0]) * KDIM, KDIM)
            term = dot(lsp[t], rhs9[pl.ds(start, KDIM), :])
            total = term if total is None else total + term
        return total

    @pl.loop(0, 2)
    def _(r):
        scol[...] = conv(r, list(range(9)), r * (3 * KDIM))
        pack_frame(
            lambda f, start: scol[pl.ds(start, 16), f * LANES : (f + 1) * LANES], SPA + r
        )
        a2a_send(SPA + r)

        @pl.when(r == 0)
        def _():
            a2a_send(LAT + 1)

    a2a_send(COT + 1)

    for i in range(3):
        prepare(wat[i].T, lqkv.at[pl.ds(i * C, C)])
    for i in range(4):
        prepare(wat[i], lat_b.at[i])
    prepare(wat[3].T, lout_f)
    for k in range(3):
        prepare(wte[2 - k], lte_b.at[k])

    half = LANES
    same = (iota((half, 2 * half), 0) & 7) == (iota((half, 2 * half), 1) & 7)
    scale = HEAD_DIM ** (-0.5)

    def temporal(x, h):
        lanes = pl.ds(h * half, half)
        put3(rhs3.at[0], 0, lanes, jnp.where(lane < 8, 0.0, roll(x, 8)))
        put3(rhs3.at[1], 0, lanes, x)
        put3(rhs3.at[2], 0, lanes, jnp.where(lane >= half - 8, 0.0, roll(x, half - 8)))

    def temporal_mix(weights):
        return (
            dot(weights[0], rhs3[0]) + dot(weights[1], rhs3[1]) + dot(weights[2], rhs3[2])
        )

    def twice(k):
        return jnp.concatenate([bcast[k], bcast[k]], axis=1)

    def stacked(x):
        hi, lo = x
        return jnp.concatenate([hi, lo, hi], axis=0)

    def turned(x):
        hi, lo = x
        return jnp.concatenate([hi, hi, lo], axis=0).T

    def diagonal(x):
        return jnp.concatenate([x[:half, :half], x[half:, half:]], axis=1)

    def both_ways(x):
        hi, lo = split(x)
        rows = jnp.concatenate([hi, lo], axis=0)
        cols = [
            jnp.concatenate([hi[:, h * half : (h + 1) * half], lo[:, h * half : (h + 1) * half]], axis=1)
            for h in range(2)
        ]
        return rows, jnp.concatenate(cols, axis=0)

    def pair(x):
        hi, lo = x
        zero = jnp.zeros((HEAD_DIM, half), BF16)
        parts = []
        for h in range(2):
            a, b = hi[:, h * half : (h + 1) * half], lo[:, h * half : (h + 1) * half]
            parts.append(jnp.concatenate([a, a], axis=1))
            parts.append(jnp.concatenate([b, zero], axis=1))
        return jnp.concatenate(parts, axis=0)

    def folded(x):
        d = HEAD_DIM
        return jnp.concatenate(
            [x[:d, :half] + x[d : 2 * d, :half], x[2 * d : 3 * d, half:] + x[3 * d :, half:]],
            axis=1,
        )

    @pl.loop(0, 2)
    def _(r):
        a2a_wait(LAT + r)
        unpack_col(LAT + r, lcol)
        a2a_wait(SPA + r)
        unpack_col(SPA + r, scol)
        for h in range(2):
            temporal(scol[:, h * half : (h + 1) * half], h)
        hidden = lcol[...] + temporal_mix(lte_f)
        hcol[r] = hidden
        centered = hidden - jnp.sum(hidden, axis=0, keepdims=True) * (1.0 / C)
        spread_ = jnp.sum(centered * centered, axis=0, keepdims=True) * (1.0 / C)
        ln_rstd = lax.rsqrt(spread_ + EPSILON)
        normal = centered * ln_rstd
        lcol[...] = normal
        normed = normal * twice(6) + twice(7)
        for h in range(2):
            put3(rhs1, 0, pl.ds(h * half, half), normed[:, h * half : (h + 1) * half])
        qkv[...] = dot(lqkv[...], rhs1[...])

        a2a_wait(COT + r)
        unpack_col(COT + r, gcol)
        for h in range(2):
            put3(rhs1, 0, pl.ds(h * half, half), gcol[:, h * half : (h + 1) * half])
        scol[...] = dot(lat_b[3], rhs1[...])

        for head in range(HEADS):
            rows = slice(head * HEAD_DIM, (head + 1) * HEAD_DIM)
            q = split(qkv[rows, :])
            k = split(qkv[C + head * HEAD_DIM : C + (head + 1) * HEAD_DIM, :])
            v = split(qkv[2 * C + head * HEAD_DIM : 2 * C + (head + 1) * HEAD_DIM, :])
            g = split(scol[rows, :])
            scores = jnp.where(same, diagonal(dot(turned(k), stacked(q))) * scale, -1e30)
            e = jnp.exp(scores - jnp.max(scores, axis=0, keepdims=True))
            p = e * (1.0 / jnp.sum(e, axis=0, keepdims=True))
            gp = diagonal(dot(turned(v), stacked(g)))
            gs = p * (gp - jnp.sum(p * gp, axis=0, keepdims=True)) * scale
            p_rows, p_cols = both_ways(p)
            s_rows, s_cols = both_ways(gs)
            acol[r, rows, :] = folded(dot(pair(v), p_rows))
            dqkv[0, rows, :] = folded(dot(pair(k), s_rows))
            dqkv[1, rows, :] = folded(dot_nt(pair(q), s_cols))
            dqkv[2, rows, :] = folded(dot_nt(pair(g), p_cols))

        for i in range(3):
            for h in range(2):
                put3(
                    rhs3.at[i], 0, pl.ds(h * half, half), dqkv[i, :, h * half : (h + 1) * half]
                )
        scaled = temporal_mix(lat_b) * twice(6)
        normal = lcol[...]
        first = jnp.sum(scaled, axis=0, keepdims=True) * (1.0 / C)
        second = jnp.sum(scaled * normal, axis=0, keepdims=True) * (1.0 / C)
        gcol[...] = gcol[...] + ln_rstd * (scaled - first - normal * second)
        for h in range(2):
            temporal(gcol[:, h * half : (h + 1) * half], h)
        scol[...] = temporal_mix(lte_b)
        pack_col(scol, GSP + r)
        a2a_send(GSP + r)
        pack_col(gcol, GHI + r)
        a2a_send(GHI + r)

    @pl.loop(0, 2)
    def _(r):
        for h in range(2):
            put3(rhs1, 0, pl.ds(h * half, half), acol[r, :, h * half : (h + 1) * half])
        scol[...] = hcol[r] + dot(lout_f[...], rhs1[...])
        pack_col(scol, OUT + r)
        a2a_send(OUT + r)

    @pl.loop(0, 9)
    def _(t):
        prepare(wsp[8 - t], lsp.at[t])

    gs_up, gs_down = halo_copies(gs4, 2)

    def store_gs(r):
        def store(f, start, x):
            gs4[1 + r, f, pl.ds(start, 16), :] = x

        return store

    a2a_wait(GSP)
    unpack_frame(GSP, store_gs(0))
    gs_down.start()
    a2a_wait(GSP + 1)
    unpack_frame(GSP + 1, store_gs(1))
    gs_up.start()

    @pl.loop(1, 3)
    def _(r4):
        for f in range(2):
            shifted_rhs(r4, f, gs4[r4, f])

    gact[0] = conv(0, list(range(3, 9)), 3 * KDIM)
    gact[1] = conv(1, list(range(0, 6)), 3 * KDIM)

    def store_hid(r):
        def store(f, start, x):
            ghid[r, f, pl.ds(start, 16), :] = x

        return store

    def store_out(r):
        def store(f, start, x):
            output[f, r, pl.ds(start, 16), :] = x

        return store

    for r in range(2):
        a2a_wait(GHI + r)
        unpack_frame(GHI + r, store_hid(r))

    gs_up.wait_recv()
    gs_down.wait_recv()
    for r4 in (0, 3):
        for f in range(2):
            shifted_rhs(r4, f, jnp.where(inside(r4), gs4[r4, f], 0.0))
    gact[0] = gact[0] + conv(0, list(range(0, 3)), 0)
    gact[1] = gact[1] + conv(1, list(range(6, 9)), 9 * KDIM)

    parts = []
    for f in range(2):
        lanes = slice(f * LANES, (f + 1) * LANES)
        a = gact[0, :, lanes] * fac_s[1, f]
        b = gact[1, :, lanes] * fac_s[2, f]
        gact[0, :, lanes] = a
        gact[1, :, lanes] = b
        parts.append((a + b, a * hat_s[1, f] + b * hat_s[2, f]))
    pack_stats(1, [parts[0][0], parts[1][0], parts[0][1], parts[1][1]])
    send_stats(1)

    for r in range(2):
        a2a_wait(OUT + r)
        unpack_frame(OUT + r, store_out(r))

    spread(total_stats(1), 4)
    for r in range(2):
        for f in range(2):
            grad_latent[f, r] = ghid[r, f] + bcast[2 + f] * (
                gact[r, :, f * LANES : (f + 1) * LANES]
                - bcast[4 + f]
                - hat_s[1 + r, f] * bcast[6 + f]
            )

    for t in range(12):
        bytes_wait(sbuf.at[t, pl.ds(0, n_frame - 1)], ssem.at[t])
    for copy in (lat_up, lat_down, gs_up, gs_down):
        copy.wait_send()
    for which in range(2):
        bytes_wait(stat_r.at[which, pl.ds(0, n_row - 1)], stat_ss.at[which])


def per_device(
    n_frame,
    n_row,
    latent,
    cotangent,
    gn_gain,
    gn_bias,
    w_spatial,
    w_temporal,
    ln_gain,
    ln_bias,
    w_query,
    w_key,
    w_value,
    w_out,
):
    frames, rows, chans, cols = latent.shape
    anywhere = pl.BlockSpec(memory_space=pl.ANY)
    inside = pl.BlockSpec(memory_space=pltpu.VMEM)
    vm = pltpu.VMEM
    dma = pltpu.SemaphoreType.DMA
    result = pl.pallas_call(
        functools.partial(kernel, n_frame, n_row),
        out_shape=jax.ShapeDtypeStruct((2,) + latent.shape, F32),
        in_specs=[anywhere, anywhere] + [inside] * 4 + [anywhere] * 6,
        out_specs=inside,
        scratch_shapes=[
            vm((4, 2, C, LANES), F32),
            vm((2, 2, C, LANES), F32),
            vm((4, 2, C, LANES), F32),
            vm((4, 2, C, LANES), F32),
            vm((4, 2, C, LANES), F32),
            vm((2, 2, C, LANES), F32),
            vm((2, C, 256), F32),
            vm((9, C, C), F32),
            vm((3, C, C), F32),
            vm((4, C, C), F32),
            vm((9, C, KDIM), BF16),
            vm((3, C, KDIM), BF16),
            vm((3, C, KDIM), BF16),
            vm((3 * C, KDIM), BF16),
            vm((4, C, KDIM), BF16),
            vm((C, KDIM), BF16),
            vm((12 * KDIM, 256), BF16),
            vm((3, KDIM, 256), BF16),
            vm((KDIM, 256), BF16),
            vm((12, 8, QUARTER, LANES), F32),
            vm((12, 8, QUARTER, LANES), F32),
            vm((2, 8, LANES), F32),
            vm((2, n_row, 8, LANES), F32),
            vm((8, C, LANES), F32),
            vm((C, 256), F32),
            vm((C, 256), F32),
            vm((3 * C, 256), F32),
            vm((C, 256), F32),
            vm((2, C, 256), F32),
            vm((2, C, 256), F32),
            vm((3, C, 256), F32),
            dma((14,)),
            dma((12,)),
            dma((12,)),
            dma((4,)),
            dma((4,)),
            dma((2,)),
            dma((2,)),
        ],
        compiler_params=pltpu.CompilerParams(
            collective_id=0, has_side_effects=True, vmem_limit_bytes=62 * 1024 * 1024
        ),
        cost_estimate=pl.CostEstimate(flops=10**10, bytes_accessed=10**7, transcendentals=10**6),
    )(
        latent,
        cotangent,
        gn_gain,
        gn_bias,
        ln_gain,
        ln_bias,
        w_spatial.reshape(9, C, C),
        w_temporal,
        w_query,
        w_key,
        w_value,
        w_out,
    )
    return result[0], result[1]


def solution(mesh):
    sizes = dict(mesh.shape)
    return jax.shard_map(
        functools.partial(per_device, sizes["frame"], sizes["row"]),
        mesh=mesh,
        in_specs=(P("frame", "row", None, None), P("frame", "row", None, None))
        + (P(),) * 10,
        out_specs=(P("frame", "row", None, None), P("frame", "row", None, None)),
        check_vma=False,
    )
```

```python
import functools

import jax
import jax.numpy as jnp
from jax import lax
from jax.experimental import pallas as pl
from jax.experimental.pallas import tpu as pltpu
from jax.sharding import PartitionSpec as P

C = 320
GROUPS = 32
PER_GROUP = C // GROUPS
HEADS = 5
HEAD_DIM = 64
EPSILON = 1e-05
LANES = 128
KDIM = 1024
QUARTER = C // 4
F32 = jnp.float32
BF16 = jnp.bfloat16
HIGHEST = lax.Precision.HIGHEST
MESH = pl.DeviceIdType.MESH
NT = (((1,), (1,)), ((), ()))

LAT, COT, SPA, GSP, GHI, OUT = 0, 2, 4, 6, 8, 10


def iota(shape, dim):
    return lax.broadcasted_iota(jnp.int32, shape, dim)


def roll(x, shift):
    shift = shift % x.shape[1]
    return x if shift == 0 else pltpu.roll(x, shift, 1)


def dot(a, b):
    return jnp.dot(a, b, preferred_element_type=F32)


def dot_nt(a, b):
    return lax.dot_general(a, b, NT, preferred_element_type=F32)


def exact_nt(a, b):
    return lax.dot_general(a, b, NT, precision=HIGHEST, preferred_element_type=F32)


def split(x):
    hi = x.astype(BF16)
    lo = (x - hi.astype(F32)).astype(BF16)
    return hi, lo


def transpose_chunks(xs):
    lane = iota(xs[0].shape, 1)
    bits = [(lane & (16 << i)) != 0 for i in range(3)]
    ys = [roll(x, 16 * m) for m, x in enumerate(xs)]
    out = []
    for j in range(8):
        level = [ys[(p - j) % 8] for p in range(8)]
        for bit in bits:
            level = [
                jnp.where(bit, level[2 * i + 1], level[2 * i]) for i in range(len(level) // 2)
            ]
        out.append(roll(level[0], -16 * j))
    return out


def interleave(x0, x1):
    low = (iota(x0.shape, 1) & 8) == 0
    return jnp.where(low, x0, roll(x1, 8)), jnp.where(low, roll(x0, -8), x1)


def put3(ref, base, lanes, x):
    hi, lo = split(x)
    ref[pl.ds(base, 256), lanes] = hi[:256]
    ref[pl.ds(base + 256, 256), lanes] = lo[:256]
    ref[pl.ds(base + 512, 256), lanes] = hi[:256]
    ref[pl.ds(base + 768, 64), lanes] = hi[256:]
    ref[pl.ds(base + 832, 64), lanes] = lo[256:]
    ref[pl.ds(base + 896, 64), lanes] = hi[256:]


def prepare(w, ref):
    hi = w.astype(BF16).astype(F32)
    lo = w - hi
    ref[:, 0:256] = hi[:, :256].astype(BF16)
    ref[:, 256:512] = hi[:, :256].astype(BF16)
    ref[:, 512:768] = lo[:, :256].astype(BF16)
    ref[:, 768:896] = jnp.concatenate([hi[:, 256:], hi[:, 256:]], axis=1).astype(BF16)
    ref[:, 896:1024] = jnp.concatenate([lo[:, 256:], jnp.zeros((C, 64), F32)], axis=1).astype(BF16)


def kernel(
    n_frame,
    n_row,
    latent,
    cotangent,
    vec0,
    vec1,
    vec2,
    vec3,
    w_spatial,
    w_temporal,
    w_query,
    w_key,
    w_value,
    w_out,
    result,
    res_v,
    lat4,
    cot_own,
    gs4,
    hat_s,
    fac_s,
    ghid,
    gact,
    share,
    wsp,
    wte,
    wat,
    lsp,
    lte_f,
    lte_b,
    lqkv,
    lat_b,
    lout_f,
    rhs9,
    rhs3,
    rhs1,
    sbuf,
    rbuf,
    stat_s,
    stat_r,
    bcast,
    lcol,
    scol,
    qkv,
    gcol,
    acol,
    hcol,
    dqkv,
    load_sem,
    store_sem,
    ssem,
    rsem,
    halo_s,
    halo_r,
    stat_ss,
    stat_rs,
):
    fi = lax.axis_index("frame")
    ri = lax.axis_index("row")
    members = 2 * n_row * PER_GROUP * LANES
    has_low = ri > 0
    has_high = ri < n_row - 1

    loads = []
    for r in range(2):
        for f in range(2):
            loads.append((latent.at[f, r], lat4.at[1 + r, f]))
    for r in range(2):
        for f in range(2):
            loads.append((cotangent.at[f, r], cot_own.at[r, f]))
    loads.append((w_spatial, wsp))
    loads.append((w_temporal, wte))
    for i, w in enumerate((w_query, w_key, w_value, w_out)):
        loads.append((w, wat.at[i]))
    copies = [
        pltpu.make_async_copy(src, dst, load_sem.at[i]) for i, (src, dst) in enumerate(loads)
    ]
    for c in copies[:8]:
        c.start()

    stores = [
        pltpu.make_async_copy(res_v.at[i, f, r], result.at[i, f, r], store_sem.at[4 * i + 2 * r + f])
        for i in range(2)
        for r in range(2)
        for f in range(2)
    ]
    barrier = pltpu.get_barrier_semaphore()

    @pl.loop(1, n_row)
    def _(k):
        pl.semaphore_signal(
            barrier, inc=1, device_id={"row": lax.rem(ri + k, n_row)}, device_id_type=MESH
        )

    @pl.loop(1, n_frame)
    def _(k):
        pl.semaphore_signal(
            barrier, inc=1, device_id={"frame": lax.rem(fi + k, n_frame)}, device_id_type=MESH
        )

    def a2a_send(t):
        @pl.loop(1, n_frame)
        def _(k):
            dest = lax.rem(fi + k, n_frame)
            pltpu.make_async_remote_copy(
                src_ref=sbuf.at[t, dest],
                dst_ref=rbuf.at[t, fi],
                send_sem=ssem.at[t],
                recv_sem=rsem.at[t],
                device_id={"frame": dest},
                device_id_type=MESH,
            ).start()

        rbuf[t, fi] = sbuf[t, fi]

    def bytes_wait(ref, sem):
        pltpu.make_async_copy(ref, ref, sem).wait()

    def a2a_wait(t):
        bytes_wait(rbuf.at[t, pl.ds(0, n_frame - 1)], rsem.at[t])

    def pack_frame(src, t):
        @pl.loop(0, 5, unroll=5)
        def _(i):
            xs = []
            for q in range(4):
                start = pl.multiple_of(q * QUARTER + i * 16, 16)
                xs.extend(interleave(src(0, start), src(1, start)))
            for j, x in enumerate(transpose_chunks(xs)):
                sbuf[t, j, pl.ds(pl.multiple_of(i * 16, 16), 16), :] = x

    def unpack_frame(t, store):
        @pl.loop(0, 5, unroll=5)
        def _(i):
            at = pl.ds(pl.multiple_of(i * 16, 16), 16)
            ys = transpose_chunks([rbuf[t, j, at, :] for j in range(8)])
            for q in range(4):
                x0, x1 = interleave(ys[2 * q], ys[2 * q + 1])
                start = pl.multiple_of(q * QUARTER + i * 16, 16)
                store(0, start, x0)
                store(1, start, x1)

    def pack_col(src, t):
        @pl.loop(0, 5, unroll=5)
        def _(i):
            xs = []
            for q in range(4):
                start = pl.multiple_of(q * QUARTER + i * 16, 16)
                for h in range(2):
                    xs.append(src[pl.ds(start, 16), h * LANES : (h + 1) * LANES])
            for s, x in enumerate(transpose_chunks(xs)):
                sbuf[t, s, pl.ds(pl.multiple_of(i * 16, 16), 16), :] = x

    def unpack_col(t, dst):
        @pl.loop(0, 5, unroll=5)
        def _(i):
            at = pl.ds(pl.multiple_of(i * 16, 16), 16)
            ys = transpose_chunks([rbuf[t, s, at, :] for s in range(8)])
            for q in range(4):
                start = pl.multiple_of(q * QUARTER + i * 16, 16)
                for h in range(2):
                    dst[pl.ds(start, 16), h * LANES : (h + 1) * LANES] = ys[2 * q + h]

    chan = iota((C, LANES), 0)
    first = (iota((C, LANES), 1) & (GROUPS - 1)) * PER_GROUP
    member = ((chan >= first) & (chan < first + PER_GROUP)).astype(F32)
    own_chunk = (iota((8, LANES), 1) // GROUPS) == iota((8, LANES), 0)

    def pack_stats(which, parts):
        total = jnp.zeros((8, C), F32)
        at = iota((8, LANES), 0)
        for k, part in enumerate(parts):
            total = total + exact_nt((at == k).astype(F32), part)
        tile = jnp.dot(total, member, precision=HIGHEST, preferred_element_type=F32)
        row = jnp.sum(jnp.where(own_chunk, tile, 0.0), axis=0, keepdims=True)
        stat_s[which] = jnp.broadcast_to(row, (8, LANES))
        stat_r[which, ri, pl.ds(0, 1), :] = row

    def send_stats(which):
        @pl.loop(1, n_row)
        def _(k):
            pltpu.make_async_remote_copy(
                src_ref=stat_s.at[which, pl.ds(0, 1)],
                dst_ref=stat_r.at[which, ri, pl.ds(0, 1)],
                send_sem=stat_ss.at[which],
                recv_sem=stat_rs.at[which],
                device_id={"row": lax.rem(ri + k, n_row)},
                device_id_type=MESH,
            ).start()

    def stats_wait(which, sems):
        bytes_wait(stat_r.at[which, pl.ds(0, n_row - 1), pl.ds(0, 1)], sems.at[which])

    def total_stats(which):
        stats_wait(which, stat_rs)
        total = jnp.sum(stat_r[which, :, 0:1, :], axis=0) * (1.0 / members)
        return jnp.broadcast_to(total, (8, LANES))

    def spread(row, at):
        cols = exact_nt(member, jnp.where(own_chunk, row, 0.0))
        for k in range(4):
            bcast[at + k] = jnp.broadcast_to(cols[:, k : k + 1], (C, LANES))

    def halo_copies(buf, which):
        up = pltpu.make_async_remote_copy(
            src_ref=buf.at[2],
            dst_ref=buf.at[0],
            send_sem=halo_s.at[which],
            recv_sem=halo_r.at[which],
            device_id={"row": lax.rem(ri + 1, n_row)},
            device_id_type=MESH,
        )
        down = pltpu.make_async_remote_copy(
            src_ref=buf.at[1],
            dst_ref=buf.at[3],
            send_sem=halo_s.at[which + 1],
            recv_sem=halo_r.at[which + 1],
            device_id={"row": lax.rem(ri + n_row - 1, n_row)},
            device_id_type=MESH,
        )
        return up, down

    def on(condition, action):
        pl.when(condition)(lambda: action())

    for c in copies[:4]:
        c.wait()
    for c in copies[8:]:
        c.start()
    parts = []
    for f in range(2):
        a, b = lat4[1, f], lat4[2, f]
        parts.append(a + b)
    for f in range(2):
        a, b = lat4[1, f], lat4[2, f]
        parts.append(a * a + b * b)
    pack_stats(0, parts)

    def pack_latent(r):
        pack_frame(lambda f, start: lat4[1 + r, f, pl.ds(start, 16), :], LAT + r)

    def pack_cotangent(r):
        pack_frame(lambda f, start: cot_own[r, f, pl.ds(start, 16), :], COT + r)

    pack_latent(0)
    pl.semaphore_wait(barrier, n_row - 1 + n_frame - 1)
    lat_up, lat_down = halo_copies(lat4, 0)
    on(has_high, lat_up.start)
    on(has_low, lat_down.start)
    a2a_send(LAT)
    send_stats(0)
    pack_latent(1)
    a2a_send(LAT + 1)
    for c in copies[4:8]:
        c.wait()
    pack_cotangent(0)
    pack_cotangent(1)

    for c in copies[8:]:
        c.wait()

    @pl.loop(0, 9)
    def _(t):
        prepare(wsp[t].T, lsp.at[t])

    @pl.loop(0, 3)
    def _(t):
        prepare(wte[t].T, lte_f.at[t])

    @pl.loop(0, 12)
    def _(t):
        rhs9[pl.ds(pl.multiple_of(t * KDIM + 960, 64), 64), :] = jnp.zeros((64, 256), BF16)

    for t in range(3):
        rhs3[t, pl.ds(960, 64), :] = jnp.zeros((64, 256), BF16)
    rhs1[pl.ds(960, 64), :] = jnp.zeros((64, 256), BF16)

    eye = (iota((C, C), 0) == iota((C, C), 1)).astype(F32)
    vecs = [v[...].reshape(1, C) for v in (vec0, vec1, vec2, vec3)] + [jnp.zeros((4, C), F32)]
    cols = exact_nt(eye, jnp.concatenate(vecs, axis=0))
    for k in range(4):
        bcast[4 + k] = jnp.broadcast_to(cols[:, k : k + 1], (C, LANES))

    mean2 = total_stats(0)
    a2a_send(COT)
    is_mean = iota((8, LANES), 1) < 2 * GROUPS
    var = roll(mean2, 2 * GROUPS) - mean2 * mean2
    rstd = lax.rsqrt(jnp.where(is_mean, var, 1.0) + EPSILON)
    spread(jnp.where(is_mean, mean2, roll(rstd, 2 * GROUPS)), 0)

    lane = iota((C, LANES), 1)

    def shifted_rhs(r4, f, x):
        for b in range(3):
            if b == 0:
                y = jnp.where(lane == 0, 0.0, roll(x, 1))
            elif b == 1:
                y = x
            else:
                y = jnp.where(lane == LANES - 1, 0.0, roll(x, LANES - 1))
            base = pl.multiple_of((r4 * 3 + b) * KDIM, KDIM)
            put3(rhs9, base, pl.ds(f * LANES, LANES), y)

    def inside(r4):
        return ((r4 > 0) | has_low) & ((r4 < 3) | has_high)

    def forward_rhs(r4):
        for f in range(2):
            hat = (lat4[r4, f] - bcast[f]) * bcast[2 + f]
            shifted = hat * bcast[4] + bcast[5]
            sigma = 1.0 / (1.0 + jnp.exp(-shifted))
            slope = sigma * (1.0 + shifted * (1.0 - sigma)) * bcast[4]
            hat_s[r4, f] = jnp.where(inside(r4), hat, 0.0)
            fac_s[r4, f] = jnp.where(inside(r4), slope, 0.0)
            shifted_rhs(r4, f, jnp.where(inside(r4), shifted * sigma, 0.0))

    def conv(taps, base):
        total = None
        for t in taps:
            start = pl.multiple_of(base + (t - taps[0]) * KDIM, KDIM)
            term = dot(lsp[t], rhs9[pl.ds(start, KDIM), :])
            total = term if total is None else total + term
        return total

    def send_spatial(r):
        pack_frame(
            lambda f, start: scol[pl.ds(start, 16), f * LANES : (f + 1) * LANES], SPA + r
        )
        a2a_send(SPA + r)

    forward_rhs(1)
    forward_rhs(2)
    own = conv(list(range(3, 9)), 3 * KDIM)
    on(has_low, lat_up.wait_recv)
    forward_rhs(0)
    scol[...] = own + conv(list(range(0, 3)), 0)
    send_spatial(0)
    own = conv(list(range(0, 6)), 3 * KDIM)
    on(has_high, lat_down.wait_recv)
    forward_rhs(3)
    scol[...] = own + conv(list(range(6, 9)), 9 * KDIM)
    send_spatial(1)

    for i in range(3):
        prepare(wat[i].T, lqkv.at[pl.ds(i * C, C)])
    for i in range(4):
        prepare(wat[i], lat_b.at[i])
    prepare(wat[3].T, lout_f)
    for k in range(3):
        prepare(wte[2 - k], lte_b.at[k])

    half = LANES
    same = (iota((half, 2 * half), 0) & 7) == (iota((half, 2 * half), 1) & 7)
    scale = HEAD_DIM ** (-0.5)

    def temporal(x, h):
        lanes = pl.ds(h * half, half)
        put3(rhs3.at[0], 0, lanes, jnp.where(lane < 8, 0.0, roll(x, 8)))
        put3(rhs3.at[1], 0, lanes, x)
        put3(rhs3.at[2], 0, lanes, jnp.where(lane >= half - 8, 0.0, roll(x, half - 8)))

    def temporal_mix(weights):
        return (
            dot(weights[0], rhs3[0]) + dot(weights[1], rhs3[1]) + dot(weights[2], rhs3[2])
        )

    def twice(k):
        return jnp.concatenate([bcast[k], bcast[k]], axis=1)

    def stacked(x):
        hi, lo = x
        return jnp.concatenate([hi, lo, hi], axis=0)

    def turned(x):
        hi, lo = x
        return jnp.concatenate([hi, hi, lo], axis=0).T

    def diagonal(x):
        return jnp.concatenate([x[:half, :half], x[half:, half:]], axis=1)

    def both_ways(x):
        hi, lo = split(x)
        rows = jnp.concatenate([hi, lo], axis=0)
        cols = [
            jnp.concatenate([hi[:, h * half : (h + 1) * half], lo[:, h * half : (h + 1) * half]], axis=1)
            for h in range(2)
        ]
        return rows, jnp.concatenate(cols, axis=0)

    def pair(x):
        hi, lo = x
        zero = jnp.zeros((HEAD_DIM, half), BF16)
        parts = []
        for h in range(2):
            a, b = hi[:, h * half : (h + 1) * half], lo[:, h * half : (h + 1) * half]
            parts.append(jnp.concatenate([a, a], axis=1))
            parts.append(jnp.concatenate([b, zero], axis=1))
        return jnp.concatenate(parts, axis=0)

    def folded(x):
        d = HEAD_DIM
        return jnp.concatenate(
            [x[:d, :half] + x[d : 2 * d, :half], x[2 * d : 3 * d, half:] + x[3 * d :, half:]],
            axis=1,
        )

    @pl.loop(0, 2)
    def _(r):
        a2a_wait(LAT + r)
        unpack_col(LAT + r, lcol)
        a2a_wait(SPA + r)

        @pl.when(r == 0)
        def _():
            a2a_send(COT + 1)

        unpack_col(SPA + r, scol)
        for h in range(2):
            temporal(scol[:, h * half : (h + 1) * half], h)
        hidden = lcol[...] + temporal_mix(lte_f)
        hcol[r] = hidden
        centered = hidden - jnp.sum(hidden, axis=0, keepdims=True) * (1.0 / C)
        spread_ = jnp.sum(centered * centered, axis=0, keepdims=True) * (1.0 / C)
        ln_rstd = lax.rsqrt(spread_ + EPSILON)
        normal = centered * ln_rstd
        lcol[...] = normal
        normed = normal * twice(6) + twice(7)
        for h in range(2):
            put3(rhs1, 0, pl.ds(h * half, half), normed[:, h * half : (h + 1) * half])
        qkv[...] = dot(lqkv[...], rhs1[...])

        a2a_wait(COT + r)
        unpack_col(COT + r, gcol)
        for h in range(2):
            put3(rhs1, 0, pl.ds(h * half, half), gcol[:, h * half : (h + 1) * half])
        scol[...] = dot(lat_b[3], rhs1[...])

        for head in range(HEADS):
            rows = slice(head * HEAD_DIM, (head + 1) * HEAD_DIM)
            q = split(qkv[rows, :])
            k = split(qkv[C + head * HEAD_DIM : C + (head + 1) * HEAD_DIM, :])
            v = split(qkv[2 * C + head * HEAD_DIM : 2 * C + (head + 1) * HEAD_DIM, :])
            g = split(scol[rows, :])
            scores = jnp.where(same, diagonal(dot(turned(k), stacked(q))) * scale, -1e30)
            e = jnp.exp(scores - jnp.max(scores, axis=0, keepdims=True))
            p = e * (1.0 / jnp.sum(e, axis=0, keepdims=True))
            gp = diagonal(dot(turned(v), stacked(g)))
            gs = p * (gp - jnp.sum(p * gp, axis=0, keepdims=True)) * scale
            p_rows, p_cols = both_ways(p)
            s_rows, s_cols = both_ways(gs)
            acol[r, rows, :] = folded(dot(pair(v), p_rows))
            dqkv[0, rows, :] = folded(dot(pair(k), s_rows))
            dqkv[1, rows, :] = folded(dot_nt(pair(q), s_cols))
            dqkv[2, rows, :] = folded(dot_nt(pair(g), p_cols))

        for i in range(3):
            for h in range(2):
                put3(
                    rhs3.at[i], 0, pl.ds(h * half, half), dqkv[i, :, h * half : (h + 1) * half]
                )
        scaled = temporal_mix(lat_b) * twice(6)
        normal = lcol[...]
        first = jnp.sum(scaled, axis=0, keepdims=True) * (1.0 / C)
        second = jnp.sum(scaled * normal, axis=0, keepdims=True) * (1.0 / C)
        gcol[...] = gcol[...] + ln_rstd * (scaled - first - normal * second)
        for h in range(2):
            temporal(gcol[:, h * half : (h + 1) * half], h)
        scol[...] = temporal_mix(lte_b)
        pack_col(scol, GSP + r)
        a2a_send(GSP + r)
        pack_col(gcol, GHI + r)

        @pl.when(r == 0)
        def _():
            a2a_send(GHI)


    gs_up, gs_down = halo_copies(gs4, 2)

    def store_gs(r):
        def store(f, start, x):
            gs4[1 + r, f, pl.ds(start, 16), :] = x

        return store

    def store_hid(r):
        def store(f, start, x):
            ghid[r, f, pl.ds(start, 16), :] = x

        return store

    def store_out(r):
        def store(f, start, x):
            res_v[0, f, r, pl.ds(start, 16), :] = x

        return store

    a2a_wait(GSP)
    unpack_frame(GSP, store_gs(0))
    on(has_low, gs_down.start)

    @pl.loop(0, 2)
    def _(r):
        for h in range(2):
            put3(rhs1, 0, pl.ds(h * half, half), acol[r, :, h * half : (h + 1) * half])
        scol[...] = hcol[r] + dot(lout_f[...], rhs1[...])
        pack_col(scol, OUT + r)

    a2a_send(GHI + 1)

    @pl.loop(0, 9)
    def _(t):
        prepare(wsp[8 - t], lsp.at[t])

    a2a_wait(GSP + 1)
    unpack_frame(GSP + 1, store_gs(1))
    on(has_high, gs_up.start)
    a2a_send(OUT)
    a2a_send(OUT + 1)

    def back_rhs(r4):
        for f in range(2):
            shifted_rhs(r4, f, jnp.where(inside(r4), gs4[r4, f], 0.0))

    for r4 in (1, 2):
        back_rhs(r4)
    gact[0] = conv(list(range(3, 9)), 3 * KDIM)
    gact[1] = conv(list(range(0, 6)), 3 * KDIM)
    share[0] = conv(list(range(6, 9)), 3 * KDIM)
    share[1] = conv(list(range(0, 3)), 6 * KDIM)
    sums, crosses = [], []
    for f in range(2):
        lanes = slice(f * LANES, (f + 1) * LANES)
        first = second = None
        for r4, g in ((0, share.at[0]), (1, gact.at[0]), (2, gact.at[1]), (3, share.at[1])):
            a = g[:, lanes] * fac_s[r4, f]
            b = a * hat_s[r4, f]
            first = a if first is None else first + a
            second = b if second is None else second + b
        sums.append(first)
        crosses.append(second)
    pack_stats(1, sums + crosses)
    send_stats(1)

    on(has_high, gs_down.wait_recv)
    back_rhs(3)
    gact[1] = gact[1] + conv(list(range(6, 9)), 9 * KDIM)
    on(has_low, gs_up.wait_recv)
    back_rhs(0)
    gact[0] = gact[0] + conv(list(range(0, 3)), 0)

    for r in range(2):
        a2a_wait(GHI + r)
        unpack_frame(GHI + r, store_hid(r))
    for r in range(2):
        a2a_wait(OUT + r)
        unpack_frame(OUT + r, store_out(r))
        for f in range(2):
            stores[2 * r + f].start()

    spread(total_stats(1), 4)
    for r in range(2):
        for f in range(2):
            res_v[1, f, r] = ghid[r, f] + bcast[2 + f] * (
                gact[r, :, f * LANES : (f + 1) * LANES] * fac_s[1 + r, f]
                - bcast[4 + f]
                - hat_s[1 + r, f] * bcast[6 + f]
            )
            stores[4 + 2 * r + f].start()

    for c in stores:
        c.wait()
    for t in range(12):
        bytes_wait(sbuf.at[t, pl.ds(0, n_frame - 1)], ssem.at[t])
    for up, down in ((lat_up, lat_down), (gs_up, gs_down)):
        on(has_high, up.wait_send)
        on(has_low, down.wait_send)
    for which in range(2):
        stats_wait(which, stat_ss)


def per_device(
    n_frame,
    n_row,
    latent,
    cotangent,
    gn_gain,
    gn_bias,
    w_spatial,
    w_temporal,
    ln_gain,
    ln_bias,
    w_query,
    w_key,
    w_value,
    w_out,
):
    frames, rows, chans, cols = latent.shape
    anywhere = pl.BlockSpec(memory_space=pl.ANY)
    inside = pl.BlockSpec(memory_space=pltpu.VMEM)
    vm = pltpu.VMEM
    dma = pltpu.SemaphoreType.DMA
    result = pl.pallas_call(
        functools.partial(kernel, n_frame, n_row),
        out_shape=jax.ShapeDtypeStruct((2,) + latent.shape, F32),
        in_specs=[anywhere, anywhere] + [inside] * 4 + [anywhere] * 6,
        out_specs=anywhere,
        scratch_shapes=[
            vm((2, 2, 2, C, LANES), F32),
            vm((4, 2, C, LANES), F32),
            vm((2, 2, C, LANES), F32),
            vm((4, 2, C, LANES), F32),
            vm((4, 2, C, LANES), F32),
            vm((4, 2, C, LANES), F32),
            vm((2, 2, C, LANES), F32),
            vm((2, C, 256), F32),
            vm((2, C, 256), F32),
            vm((9, C, C), F32),
            vm((3, C, C), F32),
            vm((4, C, C), F32),
            vm((9, C, KDIM), BF16),
            vm((3, C, KDIM), BF16),
            vm((3, C, KDIM), BF16),
            vm((3 * C, KDIM), BF16),
            vm((4, C, KDIM), BF16),
            vm((C, KDIM), BF16),
            vm((12 * KDIM, 256), BF16),
            vm((3, KDIM, 256), BF16),
            vm((KDIM, 256), BF16),
            vm((12, 8, QUARTER, LANES), F32),
            vm((12, 8, QUARTER, LANES), F32),
            vm((2, 8, LANES), F32),
            vm((2, n_row, 8, LANES), F32),
            vm((8, C, LANES), F32),
            vm((C, 256), F32),
            vm((C, 256), F32),
            vm((3 * C, 256), F32),
            vm((C, 256), F32),
            vm((2, C, 256), F32),
            vm((2, C, 256), F32),
            vm((3, C, 256), F32),
            dma((14,)),
            dma((8,)),
            dma((12,)),
            dma((12,)),
            dma((4,)),
            dma((4,)),
            dma((2,)),
            dma((2,)),
        ],
        compiler_params=pltpu.CompilerParams(
            collective_id=0, has_side_effects=True, vmem_limit_bytes=62 * 1024 * 1024
        ),
        cost_estimate=pl.CostEstimate(flops=10**10, bytes_accessed=10**7, transcendentals=10**6),
    )(
        latent,
        cotangent,
        gn_gain,
        gn_bias,
        ln_gain,
        ln_bias,
        w_spatial.reshape(9, C, C),
        w_temporal,
        w_query,
        w_key,
        w_value,
        w_out,
    )
    return result[0], result[1]


def solution(mesh):
    sizes = dict(mesh.shape)
    return jax.shard_map(
        functools.partial(per_device, sizes["frame"], sizes["row"]),
        mesh=mesh,
        in_specs=(P("frame", "row", None, None), P("frame", "row", None, None))
        + (P(),) * 10,
        out_specs=(P("frame", "row", None, None), P("frame", "row", None, None)),
        check_vma=False,
    )
```

```python
import functools

import jax
import jax.numpy as jnp
from jax import lax
from jax.experimental import pallas as pl
from jax.experimental.pallas import tpu as pltpu
from jax.sharding import PartitionSpec as P

C = 320
GROUPS = 32
PER_GROUP = C // GROUPS
HEADS = 5
HEAD_DIM = 64
EPSILON = 1e-05
LANES = 128
KDIM = 1024
QUARTER = C // 4
F32 = jnp.float32
BF16 = jnp.bfloat16
HIGHEST = lax.Precision.HIGHEST
MESH = pl.DeviceIdType.MESH
NT = (((1,), (1,)), ((), ()))

LAT, COT, SPA, GSP, GHI, OUT = 0, 2, 4, 6, 8, 10


def iota(shape, dim):
    return lax.broadcasted_iota(jnp.int32, shape, dim)


def roll(x, shift):
    shift = shift % x.shape[1]
    return x if shift == 0 else pltpu.roll(x, shift, 1)


def dot(a, b):
    return jnp.dot(a, b, preferred_element_type=F32)


def dot_nt(a, b):
    return lax.dot_general(a, b, NT, preferred_element_type=F32)


def exact_nt(a, b):
    return lax.dot_general(a, b, NT, precision=HIGHEST, preferred_element_type=F32)


def split(x):
    hi = x.astype(BF16)
    lo = (x - hi.astype(F32)).astype(BF16)
    return hi, lo


def transpose_chunks(xs):
    lane = iota(xs[0].shape, 1)
    bits = [(lane & (16 << i)) != 0 for i in range(3)]
    ys = [roll(x, 16 * m) for m, x in enumerate(xs)]
    out = []
    for j in range(8):
        level = [ys[(p - j) % 8] for p in range(8)]
        for bit in bits:
            level = [
                jnp.where(bit, level[2 * i + 1], level[2 * i]) for i in range(len(level) // 2)
            ]
        out.append(roll(level[0], -16 * j))
    return out


def interleave(x0, x1):
    low = (iota(x0.shape, 1) & 8) == 0
    return jnp.where(low, x0, roll(x1, 8)), jnp.where(low, roll(x0, -8), x1)


def put3(ref, base, lanes, x):
    hi, lo = split(x)
    ref[pl.ds(base, 256), lanes] = hi[:256]
    ref[pl.ds(base + 256, 256), lanes] = lo[:256]
    ref[pl.ds(base + 512, 256), lanes] = hi[:256]
    ref[pl.ds(base + 768, 64), lanes] = hi[256:]
    ref[pl.ds(base + 832, 64), lanes] = lo[256:]
    ref[pl.ds(base + 896, 64), lanes] = hi[256:]


def prepare(w, ref):
    hi = w.astype(BF16).astype(F32)
    lo = w - hi
    ref[:, 0:256] = hi[:, :256].astype(BF16)
    ref[:, 256:512] = hi[:, :256].astype(BF16)
    ref[:, 512:768] = lo[:, :256].astype(BF16)
    ref[:, 768:896] = jnp.concatenate([hi[:, 256:], hi[:, 256:]], axis=1).astype(BF16)
    ref[:, 896:1024] = jnp.concatenate([lo[:, 256:], jnp.zeros((C, 64), F32)], axis=1).astype(BF16)


def kernel(
    n_frame,
    n_row,
    latent,
    cotangent,
    vec0,
    vec1,
    vec2,
    vec3,
    w_spatial,
    w_temporal,
    w_query,
    w_key,
    w_value,
    w_out,
    result,
    res_v,
    lat4,
    cot_own,
    gs4,
    hat_s,
    fac_s,
    ghid,
    gact,
    share,
    wsp,
    wte,
    wat,
    lsp,
    lte_f,
    lte_b,
    lqkv,
    lat_b,
    lout_f,
    rhs9,
    rhs3,
    rhs1,
    sbuf,
    rbuf,
    stat_s,
    stat_r,
    bcast,
    lcol,
    scol,
    qkv,
    gcol,
    acol,
    hcol,
    dqkv,
    load_sem,
    store_sem,
    ssem,
    rsem,
    halo_s,
    halo_r,
    stat_ss,
    stat_rs,
):
    fi = lax.axis_index("frame")
    ri = lax.axis_index("row")
    members = 2 * n_row * PER_GROUP * LANES
    has_low = ri > 0
    has_high = ri < n_row - 1

    loads = []
    for r in range(2):
        for f in range(2):
            loads.append((latent.at[f, r], lat4.at[1 + r, f]))
    for r in range(2):
        for f in range(2):
            loads.append((cotangent.at[f, r], cot_own.at[r, f]))
    loads.append((w_spatial, wsp))
    loads.append((w_temporal, wte))
    for i, w in enumerate((w_query, w_key, w_value, w_out)):
        loads.append((w, wat.at[i]))
    copies = [
        pltpu.make_async_copy(src, dst, load_sem.at[i]) for i, (src, dst) in enumerate(loads)
    ]
    for c in copies[:8]:
        c.start()

    stores = [
        pltpu.make_async_copy(res_v.at[i, f, r], result.at[i, f, r], store_sem.at[4 * i + 2 * r + f])
        for i in range(2)
        for r in range(2)
        for f in range(2)
    ]
    barrier = pltpu.get_barrier_semaphore()

    @pl.loop(1, n_row)
    def _(k):
        pl.semaphore_signal(
            barrier, inc=1, device_id={"row": lax.rem(ri + k, n_row)}, device_id_type=MESH
        )

    @pl.loop(1, n_frame)
    def _(k):
        pl.semaphore_signal(
            barrier, inc=1, device_id={"frame": lax.rem(fi + k, n_frame)}, device_id_type=MESH
        )

    ring = 4 if n_frame % 4 == 0 else n_frame

    def a2a_send(t):
        @pl.loop(1, n_frame)
        def _(k):
            dest = lax.rem(fi // ring + k // ring, n_frame // ring) * ring + lax.rem(fi + k, ring)
            pltpu.make_async_remote_copy(
                src_ref=sbuf.at[t, dest],
                dst_ref=rbuf.at[t, fi],
                send_sem=ssem.at[t],
                recv_sem=rsem.at[t],
                device_id={"frame": dest},
                device_id_type=MESH,
            ).start()

        rbuf[t, fi] = sbuf[t, fi]

    def bytes_wait(ref, sem):
        pltpu.make_async_copy(ref, ref, sem).wait()

    def a2a_wait(t):
        bytes_wait(rbuf.at[t, pl.ds(0, n_frame - 1)], rsem.at[t])

    def pack_frame(src, t):
        @pl.loop(0, 5, unroll=5)
        def _(i):
            xs = []
            for q in range(4):
                start = pl.multiple_of(q * QUARTER + i * 16, 16)
                xs.extend(interleave(src(0, start), src(1, start)))
            for j, x in enumerate(transpose_chunks(xs)):
                sbuf[t, j, pl.ds(pl.multiple_of(i * 16, 16), 16), :] = x

    def unpack_frame(t, store):
        @pl.loop(0, 5, unroll=5)
        def _(i):
            at = pl.ds(pl.multiple_of(i * 16, 16), 16)
            ys = transpose_chunks([rbuf[t, j, at, :] for j in range(8)])
            for q in range(4):
                x0, x1 = interleave(ys[2 * q], ys[2 * q + 1])
                start = pl.multiple_of(q * QUARTER + i * 16, 16)
                store(0, start, x0)
                store(1, start, x1)

    def pack_col(src, t):
        @pl.loop(0, 5, unroll=5)
        def _(i):
            xs = []
            for q in range(4):
                start = pl.multiple_of(q * QUARTER + i * 16, 16)
                for h in range(2):
                    xs.append(src[pl.ds(start, 16), h * LANES : (h + 1) * LANES])
            for s, x in enumerate(transpose_chunks(xs)):
                sbuf[t, s, pl.ds(pl.multiple_of(i * 16, 16), 16), :] = x

    def unpack_col(t, dst):
        @pl.loop(0, 5, unroll=5)
        def _(i):
            at = pl.ds(pl.multiple_of(i * 16, 16), 16)
            ys = transpose_chunks([rbuf[t, s, at, :] for s in range(8)])
            for q in range(4):
                start = pl.multiple_of(q * QUARTER + i * 16, 16)
                for h in range(2):
                    dst[pl.ds(start, 16), h * LANES : (h + 1) * LANES] = ys[2 * q + h]

    chan = iota((C, LANES), 0)
    first = (iota((C, LANES), 1) & (GROUPS - 1)) * PER_GROUP
    member = ((chan >= first) & (chan < first + PER_GROUP)).astype(F32)
    own_chunk = (iota((8, LANES), 1) // GROUPS) == iota((8, LANES), 0)

    def pack_stats(which, parts):
        total = jnp.zeros((8, C), F32)
        at = iota((8, LANES), 0)
        for k, part in enumerate(parts):
            total = total + exact_nt((at == k).astype(F32), part)
        tile = jnp.dot(total, member, precision=HIGHEST, preferred_element_type=F32)
        row = jnp.sum(jnp.where(own_chunk, tile, 0.0), axis=0, keepdims=True)
        stat_s[which] = jnp.broadcast_to(row, (8, LANES))
        stat_r[which, ri, pl.ds(0, 1), :] = row

    def send_stats(which):
        @pl.loop(1, n_row)
        def _(k):
            pltpu.make_async_remote_copy(
                src_ref=stat_s.at[which, pl.ds(0, 1)],
                dst_ref=stat_r.at[which, ri, pl.ds(0, 1)],
                send_sem=stat_ss.at[which],
                recv_sem=stat_rs.at[which],
                device_id={"row": lax.rem(ri + k, n_row)},
                device_id_type=MESH,
            ).start()

    def stats_wait(which, sems):
        bytes_wait(stat_r.at[which, pl.ds(0, n_row - 1), pl.ds(0, 1)], sems.at[which])

    def total_stats(which):
        stats_wait(which, stat_rs)
        total = jnp.sum(stat_r[which, :, 0:1, :], axis=0) * (1.0 / members)
        return jnp.broadcast_to(total, (8, LANES))

    def spread(row, at):
        cols = exact_nt(member, jnp.where(own_chunk, row, 0.0))
        for k in range(4):
            bcast[at + k] = jnp.broadcast_to(cols[:, k : k + 1], (C, LANES))

    def halo_copies(buf, which):
        up = pltpu.make_async_remote_copy(
            src_ref=buf.at[2],
            dst_ref=buf.at[0],
            send_sem=halo_s.at[which],
            recv_sem=halo_r.at[which],
            device_id={"row": lax.rem(ri + 1, n_row)},
            device_id_type=MESH,
        )
        down = pltpu.make_async_remote_copy(
            src_ref=buf.at[1],
            dst_ref=buf.at[3],
            send_sem=halo_s.at[which + 1],
            recv_sem=halo_r.at[which + 1],
            device_id={"row": lax.rem(ri + n_row - 1, n_row)},
            device_id_type=MESH,
        )
        return up, down

    def on(condition, action):
        pl.when(condition)(lambda: action())

    for c in copies[:4]:
        c.wait()
    for c in copies[8:]:
        c.start()
    parts = []
    for f in range(2):
        a, b = lat4[1, f], lat4[2, f]
        parts.append(a + b)
    for f in range(2):
        a, b = lat4[1, f], lat4[2, f]
        parts.append(a * a + b * b)
    pack_stats(0, parts)

    def pack_latent(r):
        pack_frame(lambda f, start: lat4[1 + r, f, pl.ds(start, 16), :], LAT + r)

    def pack_cotangent(r):
        pack_frame(lambda f, start: cot_own[r, f, pl.ds(start, 16), :], COT + r)

    pack_latent(0)
    pl.semaphore_wait(barrier, n_row - 1 + n_frame - 1)
    lat_up, lat_down = halo_copies(lat4, 0)
    on(has_high, lat_up.start)
    on(has_low, lat_down.start)
    send_stats(0)
    a2a_send(LAT)
    pack_latent(1)
    a2a_send(LAT + 1)
    for c in copies[4:8]:
        c.wait()
    pack_cotangent(0)
    pack_cotangent(1)

    for c in copies[8:]:
        c.wait()

    @pl.loop(0, 9)
    def _(t):
        prepare(wsp[t].T, lsp.at[t])

    @pl.loop(0, 3)
    def _(t):
        prepare(wte[t].T, lte_f.at[t])

    @pl.loop(0, 12)
    def _(t):
        rhs9[pl.ds(pl.multiple_of(t * KDIM + 960, 64), 64), :] = jnp.zeros((64, 256), BF16)

    for t in range(3):
        rhs3[t, pl.ds(960, 64), :] = jnp.zeros((64, 256), BF16)
    rhs1[pl.ds(960, 64), :] = jnp.zeros((64, 256), BF16)

    eye = (iota((C, C), 0) == iota((C, C), 1)).astype(F32)
    vecs = [v[...].reshape(1, C) for v in (vec0, vec1, vec2, vec3)] + [jnp.zeros((4, C), F32)]
    cols = exact_nt(eye, jnp.concatenate(vecs, axis=0))
    for k in range(4):
        bcast[4 + k] = jnp.broadcast_to(cols[:, k : k + 1], (C, LANES))

    mean2 = total_stats(0)
    a2a_send(COT)
    is_mean = iota((8, LANES), 1) < 2 * GROUPS
    var = roll(mean2, 2 * GROUPS) - mean2 * mean2
    rstd = lax.rsqrt(jnp.where(is_mean, var, 1.0) + EPSILON)
    spread(jnp.where(is_mean, mean2, roll(rstd, 2 * GROUPS)), 0)

    lane = iota((C, LANES), 1)

    def shifted_rhs(r4, f, x):
        for b in range(3):
            if b == 0:
                y = jnp.where(lane == 0, 0.0, roll(x, 1))
            elif b == 1:
                y = x
            else:
                y = jnp.where(lane == LANES - 1, 0.0, roll(x, LANES - 1))
            base = pl.multiple_of((r4 * 3 + b) * KDIM, KDIM)
            put3(rhs9, base, pl.ds(f * LANES, LANES), y)

    def inside(r4):
        return ((r4 > 0) | has_low) & ((r4 < 3) | has_high)

    def forward_rhs(r4):
        for f in range(2):
            hat = (lat4[r4, f] - bcast[f]) * bcast[2 + f]
            shifted = hat * bcast[4] + bcast[5]
            sigma = 1.0 / (1.0 + jnp.exp(-shifted))
            slope = sigma * (1.0 + shifted * (1.0 - sigma)) * bcast[4]
            hat_s[r4, f] = jnp.where(inside(r4), hat, 0.0)
            fac_s[r4, f] = jnp.where(inside(r4), slope, 0.0)
            shifted_rhs(r4, f, jnp.where(inside(r4), shifted * sigma, 0.0))

    def conv(taps, base):
        total = None
        for t in taps:
            start = pl.multiple_of(base + (t - taps[0]) * KDIM, KDIM)
            term = dot(lsp[t], rhs9[pl.ds(start, KDIM), :])
            total = term if total is None else total + term
        return total

    def send_spatial(r):
        pack_frame(
            lambda f, start: scol[pl.ds(start, 16), f * LANES : (f + 1) * LANES], SPA + r
        )
        a2a_send(SPA + r)

    forward_rhs(1)
    forward_rhs(2)
    own = conv(list(range(3, 9)), 3 * KDIM)
    on(has_low, lat_up.wait_recv)
    forward_rhs(0)
    scol[...] = own + conv(list(range(0, 3)), 0)
    send_spatial(0)
    own = conv(list(range(0, 6)), 3 * KDIM)
    on(has_high, lat_down.wait_recv)
    forward_rhs(3)
    scol[...] = own + conv(list(range(6, 9)), 9 * KDIM)
    send_spatial(1)

    for i in range(3):
        prepare(wat[i].T, lqkv.at[pl.ds(i * C, C)])
    for i in range(4):
        prepare(wat[i], lat_b.at[i])
    prepare(wat[3].T, lout_f)
    for k in range(3):
        prepare(wte[2 - k], lte_b.at[k])

    half = LANES
    same = (iota((half, 2 * half), 0) & 7) == (iota((half, 2 * half), 1) & 7)
    scale = HEAD_DIM ** (-0.5)

    def temporal(x, h):
        lanes = pl.ds(h * half, half)
        put3(rhs3.at[0], 0, lanes, jnp.where(lane < 8, 0.0, roll(x, 8)))
        put3(rhs3.at[1], 0, lanes, x)
        put3(rhs3.at[2], 0, lanes, jnp.where(lane >= half - 8, 0.0, roll(x, half - 8)))

    def temporal_mix(weights):
        return (
            dot(weights[0], rhs3[0]) + dot(weights[1], rhs3[1]) + dot(weights[2], rhs3[2])
        )

    def twice(k):
        return jnp.concatenate([bcast[k], bcast[k]], axis=1)

    def stacked(x):
        hi, lo = x
        return jnp.concatenate([hi, lo, hi], axis=0)

    def turned(x):
        hi, lo = x
        return jnp.concatenate([hi, hi, lo], axis=0).T

    def diagonal(x):
        return jnp.concatenate([x[:half, :half], x[half:, half:]], axis=1)

    def both_ways(x):
        hi, lo = split(x)
        rows = jnp.concatenate([hi, lo], axis=0)
        cols = [
            jnp.concatenate([hi[:, h * half : (h + 1) * half], lo[:, h * half : (h + 1) * half]], axis=1)
            for h in range(2)
        ]
        return rows, jnp.concatenate(cols, axis=0)

    def pair(x):
        hi, lo = x
        zero = jnp.zeros((HEAD_DIM, half), BF16)
        parts = []
        for h in range(2):
            a, b = hi[:, h * half : (h + 1) * half], lo[:, h * half : (h + 1) * half]
            parts.append(jnp.concatenate([a, a], axis=1))
            parts.append(jnp.concatenate([b, zero], axis=1))
        return jnp.concatenate(parts, axis=0)

    def folded(x):
        d = HEAD_DIM
        return jnp.concatenate(
            [x[:d, :half] + x[d : 2 * d, :half], x[2 * d : 3 * d, half:] + x[3 * d :, half:]],
            axis=1,
        )

    @pl.loop(0, 2)
    def _(r):
        a2a_wait(LAT + r)
        unpack_col(LAT + r, lcol)
        a2a_wait(SPA + r)

        @pl.when(r == 0)
        def _():
            a2a_send(COT + 1)

        unpack_col(SPA + r, scol)
        for h in range(2):
            temporal(scol[:, h * half : (h + 1) * half], h)
        hidden = lcol[...] + temporal_mix(lte_f)
        hcol[r] = hidden
        centered = hidden - jnp.sum(hidden, axis=0, keepdims=True) * (1.0 / C)
        spread_ = jnp.sum(centered * centered, axis=0, keepdims=True) * (1.0 / C)
        ln_rstd = lax.rsqrt(spread_ + EPSILON)
        normal = centered * ln_rstd
        lcol[...] = normal
        normed = normal * twice(6) + twice(7)
        for h in range(2):
            put3(rhs1, 0, pl.ds(h * half, half), normed[:, h * half : (h + 1) * half])
        qkv[...] = dot(lqkv[...], rhs1[...])

        a2a_wait(COT + r)
        unpack_col(COT + r, gcol)
        for h in range(2):
            put3(rhs1, 0, pl.ds(h * half, half), gcol[:, h * half : (h + 1) * half])
        scol[...] = dot(lat_b[3], rhs1[...])

        for head in range(HEADS):
            rows = slice(head * HEAD_DIM, (head + 1) * HEAD_DIM)
            q = split(qkv[rows, :])
            k = split(qkv[C + head * HEAD_DIM : C + (head + 1) * HEAD_DIM, :])
            v = split(qkv[2 * C + head * HEAD_DIM : 2 * C + (head + 1) * HEAD_DIM, :])
            g = split(scol[rows, :])
            scores = jnp.where(same, diagonal(dot(turned(k), stacked(q))) * scale, -1e30)
            e = jnp.exp(scores - jnp.max(scores, axis=0, keepdims=True))
            p = e * (1.0 / jnp.sum(e, axis=0, keepdims=True))
            gp = diagonal(dot(turned(v), stacked(g)))
            gs = p * (gp - jnp.sum(p * gp, axis=0, keepdims=True)) * scale
            p_rows, p_cols = both_ways(p)
            s_rows, s_cols = both_ways(gs)
            acol[r, rows, :] = folded(dot(pair(v), p_rows))
            dqkv[0, rows, :] = folded(dot(pair(k), s_rows))
            dqkv[1, rows, :] = folded(dot_nt(pair(q), s_cols))
            dqkv[2, rows, :] = folded(dot_nt(pair(g), p_cols))

        for i in range(3):
            for h in range(2):
                put3(
                    rhs3.at[i], 0, pl.ds(h * half, half), dqkv[i, :, h * half : (h + 1) * half]
                )
        scaled = temporal_mix(lat_b) * twice(6)
        normal = lcol[...]
        first = jnp.sum(scaled, axis=0, keepdims=True) * (1.0 / C)
        second = jnp.sum(scaled * normal, axis=0, keepdims=True) * (1.0 / C)
        gcol[...] = gcol[...] + ln_rstd * (scaled - first - normal * second)
        for h in range(2):
            temporal(gcol[:, h * half : (h + 1) * half], h)
        scol[...] = temporal_mix(lte_b)
        pack_col(scol, GSP + r)
        a2a_send(GSP + r)
        pack_col(gcol, GHI + r)

        @pl.when(r == 0)
        def _():
            a2a_send(GHI)


    gs_up, gs_down = halo_copies(gs4, 2)

    def store_gs(r):
        def store(f, start, x):
            gs4[1 + r, f, pl.ds(start, 16), :] = x

        return store

    def store_hid(r):
        def store(f, start, x):
            ghid[r, f, pl.ds(start, 16), :] = x

        return store

    def store_out(r):
        def store(f, start, x):
            res_v[0, f, r, pl.ds(start, 16), :] = x

        return store

    a2a_wait(GSP)
    unpack_frame(GSP, store_gs(0))
    on(has_low, gs_down.start)

    @pl.loop(0, 2)
    def _(r):
        for h in range(2):
            put3(rhs1, 0, pl.ds(h * half, half), acol[r, :, h * half : (h + 1) * half])
        scol[...] = hcol[r] + dot(lout_f[...], rhs1[...])
        pack_col(scol, OUT + r)
        a2a_send(OUT + r)

    a2a_send(GHI + 1)

    @pl.loop(0, 9)
    def _(t):
        prepare(wsp[8 - t], lsp.at[t])

    a2a_wait(GSP + 1)
    unpack_frame(GSP + 1, store_gs(1))
    on(has_high, gs_up.start)

    def back_rhs(r4):
        for f in range(2):
            shifted_rhs(r4, f, jnp.where(inside(r4), gs4[r4, f], 0.0))

    for r4 in (1, 2):
        back_rhs(r4)
    gact[0] = conv(list(range(3, 9)), 3 * KDIM)
    gact[1] = conv(list(range(0, 6)), 3 * KDIM)
    share[0] = conv(list(range(6, 9)), 3 * KDIM)
    share[1] = conv(list(range(0, 3)), 6 * KDIM)
    sums, crosses = [], []
    for f in range(2):
        lanes = slice(f * LANES, (f + 1) * LANES)
        first = second = None
        for r4, g in ((0, share.at[0]), (1, gact.at[0]), (2, gact.at[1]), (3, share.at[1])):
            a = g[:, lanes] * fac_s[r4, f]
            b = a * hat_s[r4, f]
            first = a if first is None else first + a
            second = b if second is None else second + b
        sums.append(first)
        crosses.append(second)
    pack_stats(1, sums + crosses)
    send_stats(1)

    on(has_high, gs_down.wait_recv)
    back_rhs(3)
    gact[1] = gact[1] + conv(list(range(6, 9)), 9 * KDIM)
    on(has_low, gs_up.wait_recv)
    back_rhs(0)
    gact[0] = gact[0] + conv(list(range(0, 3)), 0)

    for r in range(2):
        a2a_wait(GHI + r)
        unpack_frame(GHI + r, store_hid(r))
    for r in range(2):
        a2a_wait(OUT + r)
        unpack_frame(OUT + r, store_out(r))
        for f in range(2):
            stores[2 * r + f].start()

    spread(total_stats(1), 4)
    for r in range(2):
        for f in range(2):
            res_v[1, f, r] = ghid[r, f] + bcast[2 + f] * (
                gact[r, :, f * LANES : (f + 1) * LANES] * fac_s[1 + r, f]
                - bcast[4 + f]
                - hat_s[1 + r, f] * bcast[6 + f]
            )
            stores[4 + 2 * r + f].start()

    for c in stores:
        c.wait()
    for t in range(12):
        bytes_wait(sbuf.at[t, pl.ds(0, n_frame - 1)], ssem.at[t])
    for up, down in ((lat_up, lat_down), (gs_up, gs_down)):
        on(has_high, up.wait_send)
        on(has_low, down.wait_send)
    for which in range(2):
        stats_wait(which, stat_ss)


def per_device(
    n_frame,
    n_row,
    latent,
    cotangent,
    gn_gain,
    gn_bias,
    w_spatial,
    w_temporal,
    ln_gain,
    ln_bias,
    w_query,
    w_key,
    w_value,
    w_out,
):
    frames, rows, chans, cols = latent.shape
    anywhere = pl.BlockSpec(memory_space=pl.ANY)
    inside = pl.BlockSpec(memory_space=pltpu.VMEM)
    vm = pltpu.VMEM
    dma = pltpu.SemaphoreType.DMA
    result = pl.pallas_call(
        functools.partial(kernel, n_frame, n_row),
        out_shape=jax.ShapeDtypeStruct((2,) + latent.shape, F32),
        in_specs=[anywhere, anywhere] + [inside] * 4 + [anywhere] * 6,
        out_specs=anywhere,
        scratch_shapes=[
            vm((2, 2, 2, C, LANES), F32),
            vm((4, 2, C, LANES), F32),
            vm((2, 2, C, LANES), F32),
            vm((4, 2, C, LANES), F32),
            vm((4, 2, C, LANES), F32),
            vm((4, 2, C, LANES), F32),
            vm((2, 2, C, LANES), F32),
            vm((2, C, 256), F32),
            vm((2, C, 256), F32),
            vm((9, C, C), F32),
            vm((3, C, C), F32),
            vm((4, C, C), F32),
            vm((9, C, KDIM), BF16),
            vm((3, C, KDIM), BF16),
            vm((3, C, KDIM), BF16),
            vm((3 * C, KDIM), BF16),
            vm((4, C, KDIM), BF16),
            vm((C, KDIM), BF16),
            vm((12 * KDIM, 256), BF16),
            vm((3, KDIM, 256), BF16),
            vm((KDIM, 256), BF16),
            vm((12, 8, QUARTER, LANES), F32),
            vm((12, 8, QUARTER, LANES), F32),
            vm((2, 8, LANES), F32),
            vm((2, n_row, 8, LANES), F32),
            vm((8, C, LANES), F32),
            vm((C, 256), F32),
            vm((C, 256), F32),
            vm((3 * C, 256), F32),
            vm((C, 256), F32),
            vm((2, C, 256), F32),
            vm((2, C, 256), F32),
            vm((3, C, 256), F32),
            dma((14,)),
            dma((8,)),
            dma((12,)),
            dma((12,)),
            dma((4,)),
            dma((4,)),
            dma((2,)),
            dma((2,)),
        ],
        compiler_params=pltpu.CompilerParams(
            collective_id=0, has_side_effects=True, vmem_limit_bytes=62 * 1024 * 1024
        ),
        cost_estimate=pl.CostEstimate(flops=10**10, bytes_accessed=10**7, transcendentals=10**6),
    )(
        latent,
        cotangent,
        gn_gain,
        gn_bias,
        ln_gain,
        ln_bias,
        w_spatial.reshape(9, C, C),
        w_temporal,
        w_query,
        w_key,
        w_value,
        w_out,
    )
    return result[0], result[1]


def solution(mesh):
    sizes = dict(mesh.shape)
    return jax.shard_map(
        functools.partial(per_device, sizes["frame"], sizes["row"]),
        mesh=mesh,
        in_specs=(P("frame", "row", None, None), P("frame", "row", None, None))
        + (P(),) * 10,
        out_specs=(P("frame", "row", None, None), P("frame", "row", None, None)),
        check_vma=False,
    )
```
